128 devices in a mesh: inst: 16 (over x_lo, y, core), circ: 4 (over z), rad: 2 (over x_hi).
Axes of the slice: x: 4 (x_hi: 2, x_lo: 2; x = x_hi * 2 + x_lo), y: 4, z: 4, core: 2. Of those that a mesh axis runs over, the one named last changes fastest.
Arguments:
- flow_state: float32 [32, 6, 16, 128, 128], P('inst', None, 'rad', 'circ'), may hold values from -6 to 6
- pseudo_step: float32 [16, 128, 128], P('rad', 'circ'), may hold values from 0.04 to 0.16
- frequency: float32 [1], replicated, may hold values from 0.5 to 2
- flux_jac: float32 [3, 6, 6], replicated, may hold values from -2.5 to 2.5
- donor_offset: int32 [32], replicated, may hold values from 0 to 31, as said below
Outputs:
- new_state: float32 [32, 6, 16, 128, 128], P('inst', None, 'rad', 'circ')
The draws below stay inside these ranges and needn't reach their ends.
Inputs may be any that keep to these rules, and one draw needn't show every extreme that they name: `donor_offset`: both 0 and 31 occur among the instances.
All inputs are finite; a program needn't handle non-finite values.
Results may differ from the reference program's by a relative error of at most 0.0003.
Values sent between devices are 32-bit elements; how exact they have to be, the bound alone decides.
A program may use at most 128 MiB of HBM per device.

```python
import math
import jax
import jax.numpy as jnp
from jax import lax

VARS = 6
CC = 32
NA = 128
NT = 32
NR = 16
NC = 128


def draw_donor_offset(key, part):
    key = jax.random.fold_in(key, 7)
    first_key, second_key, third_key = jax.random.split(key, 3)
    shifts = jax.random.randint(first_key, (NT,), 0, CC)
    high_slot = jax.random.randint(second_key, (), 0, NT)
    low_slot = (high_slot + 1 + jax.random.randint(third_key, (), 0, NT - 1)) % NT
    shifts = shifts.at[high_slot].set(CC - 1)
    shifts = shifts.at[low_slot].set(0)
    return shifts.astype(jnp.int32)


def levels(rng, shape, cuts, smallest, largest):
    loudness = 1.0
    for axis_at, blocks in cuts:
        steps = jax.random.uniform(jax.random.fold_in(jax.random.fold_in(rng, 6), axis_at), (blocks,), jnp.float32, smallest / len(cuts), largest / len(cuts))
        loudness = loudness * jnp.repeat(jnp.exp(steps), shape[axis_at] // blocks).reshape((-1,) + (1,) * (len(shape) - 1 - axis_at))
    return loudness


def bell_draw(key, shape, spread, most, pieces=(), kind=jnp.bfloat16):
    array = spread * jax.random.normal(key, shape, jnp.float32)
    if pieces:
        array = array * levels(key, shape, pieces, -0.22, 0.18)
    return jnp.clip(array, -most, most).astype(kind)


def setup_inputs(seed: int = 0) -> dict:
    splits = jax.random.split(jax.random.key(seed), 6)
    flow_state = bell_draw(splits[0], (NT, VARS, NR, NC, NA), 1.0, 6.0, ((0, 16), (2, 2), (3, 4)), jnp.float32)
    pseudo_step = jnp.clip(jnp.exp(math.log(0.16) - 1.3862944 * jax.random.uniform(splits[1], (NR, NC, NA), jnp.float32) ** levels(splits[1], (NR, NC, NA), ((0, 2), (1, 4)), -0.2, 0.2)), 0.04, 0.16)
    frequency = jnp.clip(jnp.exp(jax.random.uniform(splits[2], (1,), jnp.float32, math.log(0.5), math.log(2.0))), 0.5, 2.0)
    flux_jac = bell_draw(splits[3], (3, VARS, VARS), VARS ** -0.5, 2.5, (), jnp.float32)
    donor_offset = draw_donor_offset(jax.random.fold_in(splits[5], 71), 0)
    return dict(flow_state=flow_state, pseudo_step=pseudo_step, frequency=frequency, flux_jac=flux_jac, donor_offset=donor_offset)


BEND = (0.3, 0.2, 0.25)
SMOOTH = (0.5, 0.5, 0.5)
PRODUCE = 0.4
DESTROY = 0.2

def spectral_table(length):
    indices = jnp.arange(length, dtype=jnp.int32)
    offset_grid = indices[:, None] - indices[None, :]
    parity = jnp.where(jnp.remainder(offset_grid, 2) == 0, 1.0, -1.0).astype(jnp.float32)
    nonzero = jnp.where(offset_grid == 0, 1, offset_grid).astype(jnp.float32)
    matrix = 0.5 * parity / jnp.tan(jnp.pi * nonzero / length)
    return jnp.where(offset_grid == 0, jnp.zeros_like(matrix), matrix)

def flux_of(current, jacobian, bend):
    linear = jnp.einsum('uv,iv...->iu...', jacobian, current, precision=lax.Precision.HIGHEST)
    return linear + 0.5 * bend * current[:, 0:1] * current

def axial_sides(current, stator_ghost, rotor_ghost):
    middle = current.shape[-1] // 2
    zero_column = jnp.zeros_like(current[..., :1])
    lower_side = jnp.concatenate([zero_column, current[..., :-1]], axis=-1)
    upper_side = jnp.concatenate([current[..., 1:], zero_column], axis=-1)
    lower_side = lower_side.at[..., middle].set(stator_ghost)
    upper_side = upper_side.at[..., middle - 1].set(rotor_ghost)
    return (lower_side, upper_side)

def spatial_residual(current, neighbours, flux_jac):
    summed = jnp.zeros_like(current)
    for axis_number in range(3):
        lower_side, upper_side = neighbours[axis_number]
        jacobian = flux_jac[axis_number]
        summed = summed + 0.5 * (flux_of(upper_side, jacobian, BEND[axis_number]) - flux_of(lower_side, jacobian, BEND[axis_number]))
        summed = summed - SMOOTH[axis_number] * (upper_side - 2.0 * current + lower_side)
    eddy_state = current[:, 5]
    source = PRODUCE * eddy_state * jnp.sqrt(1.0 + current[:, 1] ** 2 + current[:, 2] ** 2) - DESTROY * eddy_state * jnp.abs(eddy_state)
    return summed.at[:, 5].add(-source)

def donor_rows(interface, begin_at, width_cells):
    return lax.dynamic_slice_in_dim(interface, begin_at.astype(jnp.int32), width_cells, 2)

def reference(flow_state, pseudo_step, frequency, flux_jac, donor_offset):
    current = flow_state
    middle = NA // 2
    radial_pad = jnp.pad(current, ((0, 0), (0, 0), (1, 1), (0, 0), (0, 0)))
    circ_pad = jnp.concatenate([current[:, :, :, -1:], current, current[:, :, :, :1]], axis=3)
    rotor_last = current[..., middle - 1]
    stator_first = current[..., middle]
    rotor_span = jnp.concatenate([rotor_last, rotor_last], axis=3)
    stator_span = jnp.concatenate([stator_first, stator_first], axis=3)
    stator_ghost = jax.vmap(lambda interface, begin_at: donor_rows(interface, begin_at, NC))(rotor_span, donor_offset.astype(jnp.int32))
    rotor_ghost = jax.vmap(lambda interface, begin_at: donor_rows(interface, begin_at, NC))(stator_span, (NC - donor_offset).astype(jnp.int32))
    neighbours = [(radial_pad[:, :, :-2], radial_pad[:, :, 2:]), (circ_pad[:, :, :, :-2], circ_pad[:, :, :, 2:]), axial_sides(current, stator_ghost, rotor_ghost)]
    spatial = spatial_residual(current, neighbours, flux_jac)
    matrix = jnp.asarray(spectral_table(NT), dtype=jnp.float32)
    derivative = jnp.einsum('nm,m...->n...', matrix, current, precision=lax.Precision.HIGHEST)
    return current - pseudo_step * (spatial + frequency[0] * derivative)
```

```python
import functools

import jax
import jax.numpy as jnp
import numpy as np
from jax import lax
from jax.experimental import pallas as pl
from jax.experimental.pallas import tpu as pltpu
from jax.sharding import PartitionSpec as P

MESH = pl.DeviceIdType.MESH
BEND = (0.3, 0.2, 0.25)
PRODUCE = 0.4
DESTROY = 0.2
VARS = 6
TIMES = 32
LAYERS = 8
ROWS = 32
HALF = 16
LANES = 128
GROUP = 16
PAD = 8


def spectral_weights(length):
    k = np.arange(length)
    sign = np.where(k % 2 == 0, 1.0, -1.0)
    angle = np.pi * np.where(k == 0, 1, k) / length
    weights = 0.5 * sign / np.tan(angle)
    weights[0] = 0.0
    weights[length // 2] = 0.0
    return weights


def circulant(first, rows, fold):
    length = len(first)
    return [
        [first[n - m] if n >= m else fold * first[n - m + length] for m in range(length)]
        for n in range(rows)
    ]


def apply_rows(matrix, values):
    results = []
    for row in matrix:
        total = None
        for weight, value in zip(row, values):
            if abs(weight) < 1e-12:
                continue
            term = np.float32(weight) * value
            total = term if total is None else total + term
        results.append(total)
    return results


def differentiate(values):
    d = spectral_weights(TIMES)
    even = 0.5 * (d[:16] + d[16:])
    odd = 0.5 * (d[:16] - d[16:])
    even_even = 0.5 * (even[:8] + even[8:])
    even_odd = 0.5 * (even[:8] - even[8:])
    sums = [values[m] + values[m + 16] for m in range(16)]
    gaps = [values[m] - values[m + 16] for m in range(16)]
    sum_sums = [sums[m] + sums[m + 8] for m in range(8)]
    sum_gaps = [sums[m] - sums[m + 8] for m in range(8)]
    a = apply_rows(circulant(even_even, 8, 1.0), sum_sums)
    b = apply_rows(circulant(even_odd, 8, -1.0), sum_gaps)
    e = [a[n] + b[n] for n in range(8)] + [a[n] - b[n] for n in range(8)]
    o = apply_rows(circulant(odd, 16, -1.0), gaps)
    return [e[n] + o[n] for n in range(16)] + [e[n] - o[n] for n in range(16)]


def kernel(
    q, dt_hbm, freq_hbm, jac_hbm, shift_hbm, out,
    cells, step, freq, jac, shift, rows_out, rows_in, columns, ghosts,
    gathered, derived, returned, fresh,
    local_sem, out_send, out_recv, back_send, back_recv, side_send, side_recv, store_sem,
):
    me = lax.axis_index("inst")
    rad = lax.axis_index("rad")
    circ = lax.axis_index("circ")
    x, y, c = me // 8, lax.rem(me // 2, 4), lax.rem(me, 2)
    peers = []
    for dx, dy, dc in [
        (1, 2, 0), (1, 2, 1), (1, 1, 0), (1, 3, 0), (1, 1, 1), (1, 3, 1), (1, 0, 0), (1, 0, 1),
        (0, 2, 0), (0, 2, 1), (0, 1, 0), (0, 3, 0), (0, 1, 1), (0, 3, 1), (0, 0, 1),
    ]:
        peers.append((lax.rem(x + dx, 2) * 4 + lax.rem(y + dy, 4)) * 2 + lax.rem(c + dc, 2))
    after = {"circ": lax.rem(circ + 1, 4)}
    before = {"circ": lax.rem(circ + 3, 4)}
    across = {"rad": 1 - rad}

    loads = [
        pltpu.make_async_copy(
            q.at[:, :, r], cells.at[:, :, r + 1, pl.ds(PAD, ROWS)], local_sem.at[0]
        )
        for r in range(LAYERS)
    ]
    for copy in loads:
        copy.start()
    small = [
        pltpu.make_async_copy(dt_hbm, step, local_sem.at[1]),
        pltpu.make_async_copy(freq_hbm, freq, local_sem.at[2]),
        pltpu.make_async_copy(jac_hbm, jac, local_sem.at[3]),
        pltpu.make_async_copy(shift_hbm, shift, local_sem.at[4]),
        pltpu.make_async_copy(
            q.at[:, :, me // 2, pl.ds(pl.multiple_of(HALF * c, HALF), HALF)],
            gathered.at[pl.ds(2 * me, 2)], local_sem.at[5],
        ),
    ]
    for copy in small:
        copy.start()

    barrier = pltpu.get_barrier_semaphore()
    for peer in peers:
        pl.semaphore_signal(barrier, inc=1, device_id={"inst": peer}, device_id_type=MESH)
    for peer in (after, before, across):
        pl.semaphore_signal(barrier, inc=1, device_id=peer, device_id_type=MESH)
    pl.semaphore_wait(barrier, GROUP - 1 + 3)

    def send_out(v, _):
        for peer in peers:
            pltpu.make_async_remote_copy(
                q.at[:, pl.ds(v, 1), peer // 2, pl.ds(pl.multiple_of(HALF * lax.rem(peer, 2), HALF), HALF)],
                gathered.at[pl.ds(2 * me, 2), pl.ds(v, 1)],
                out_send, out_recv.at[v],
                device_id={"inst": peer}, device_id_type=MESH,
            ).start()
        return 0

    lax.fori_loop(0, VARS, send_out, 0)
    layer_copy = pltpu.make_async_remote_copy(
        q.at[:, :, (LAYERS - 1) * (1 - rad)],
        cells.at[:, :, (LAYERS + 1) * rad, pl.ds(PAD, ROWS)],
        side_send.at[0], side_recv.at[0], device_id=across, device_id_type=MESH,
    )
    layer_copy.start()

    for copy in loads:
        copy.wait()

    lane = lax.broadcasted_iota(jnp.int32, (ROWS, LANES), 1)

    def pack(n, _):
        packed = jnp.zeros((ROWS, LANES), jnp.float32)
        for v in range(VARS):
            for r in range(LAYERS):
                rows_out[0, n, v, r:r + 1] = cells[n, v, r + 1, PAD + ROWS - 1:PAD + ROWS]
                rows_out[1, n, v, r:r + 1] = cells[n, v, r + 1, PAD:PAD + 1]
                j = v * LAYERS + r
                block = pltpu.roll(cells[n, v, r + 1, PAD:PAD + ROWS], (2 * j - 63) % LANES, 1)
                packed = jnp.where(lane // 2 == j, block, packed)
        columns[n, ROWS:2 * ROWS] = packed
        return 0

    lax.fori_loop(0, 2, pack, 0)
    side_copies = [
        pltpu.make_async_remote_copy(
            rows_out.at[0], rows_in.at[0], side_send.at[1], side_recv.at[1],
            device_id=after, device_id_type=MESH,
        ),
        pltpu.make_async_remote_copy(
            rows_out.at[1], rows_in.at[1], side_send.at[2], side_recv.at[2],
            device_id=before, device_id_type=MESH,
        ),
        pltpu.make_async_remote_copy(
            columns.at[:, pl.ds(ROWS, ROWS)], columns.at[:, pl.ds(0, ROWS)],
            side_send.at[3], side_recv.at[3], device_id=after, device_id_type=MESH,
        ),
        pltpu.make_async_remote_copy(
            columns.at[:, pl.ds(ROWS, ROWS)], columns.at[:, pl.ds(2 * ROWS, ROWS)],
            side_send.at[4], side_recv.at[4], device_id=before, device_id_type=MESH,
        ),
    ]
    for copy in side_copies:
        copy.start()
    cells[:, :, (LAYERS + 1) * rad, PAD:PAD + ROWS] = jnp.zeros((2, VARS, ROWS, LANES), jnp.float32)
    for copy in small:
        copy.wait()
    for copy in side_copies:
        copy.wait_recv()

    def unpack(n, _):
        for v in range(VARS):
            for r in range(LAYERS):
                cells[n, v, r + 1, PAD - 1:PAD] = rows_in[0, n, v, r:r + 1]
                cells[n, v, r + 1, PAD + ROWS:PAD + ROWS + 1] = rows_in[1, n, v, r:r + 1]
        s = shift[2 * me + n]
        stator = columns[n, pl.ds(ROWS + s, ROWS)]
        rotor = columns[n, pl.ds(ROWS - s, ROWS)]
        ghosts[n] = jnp.where(lane % 2 == 0, pltpu.roll(rotor, LANES - 1, 1), pltpu.roll(stator, 1, 1))
        return 0

    lax.fori_loop(0, 2, unpack, 0)
    layer_copy.wait_recv()

    def spatial(t, _):
        n, r = t // LAYERS, lax.rem(t, LAYERS)
        ghost = ghosts[n]
        here, sides = [], [[], [], []]
        for v in range(VARS):
            now = cells[n, v, r + 1, PAD:PAD + ROWS]
            here.append(now)
            sides[0].append((cells[n, v, r, PAD:PAD + ROWS], cells[n, v, r + 2, PAD:PAD + ROWS]))
            sides[1].append((cells[n, v, r + 1, PAD - 1:PAD + ROWS - 1], cells[n, v, r + 1, PAD + 1:PAD + ROWS + 1]))
            first = 63 - 2 * LAYERS * v
            placed = pltpu.roll(ghost, (first if first > 2 * LAYERS - 2 else first + LANES) - 2 * r, 1)
            lower = jnp.where(lane == 64, placed, jnp.where(lane == 0, 0.0, pltpu.roll(now, 1, 1)))
            upper = jnp.where(lane == 63, placed, jnp.where(lane == LANES - 1, 0.0, pltpu.roll(now, LANES - 1, 1)))
            sides[2].append((lower, upper))
        linear = [None] * VARS
        rest = [3.0 * now for now in here]
        for d in range(3):
            low0 = (0.25 * BEND[d]) * sides[d][0][0] + 0.5
            high0 = (0.25 * BEND[d]) * sides[d][0][1] - 0.5
            for v in range(VARS):
                low, high = sides[d][v]
                rest[v] = rest[v] + (high * high0 - low * low0)
                gap = high - low
                for u in range(VARS):
                    term = jac[d, u, v] * gap
                    linear[u] = term if linear[u] is None else linear[u] + term
        eddy = here[5]
        source = PRODUCE * eddy * jnp.sqrt(1.0 + here[1] * here[1] + here[2] * here[2]) - DESTROY * eddy * jnp.abs(eddy)
        rest[5] = rest[5] - source
        pace = step[r]
        for v in range(VARS):
            fresh[n, v, r] = here[v] - pace * (rest[v] + 0.5 * linear[v])
        return 0

    lax.fori_loop(0, 2 * LAYERS, spatial, 0)

    def send_back(v, _):
        part = gathered.at[pl.ds(0, TIMES - 2), pl.ds(v, 1)]
        pltpu.make_async_copy(part, part, out_recv.at[v]).wait()
        for h in range(HALF // 8):
            values = [gathered[m, v, 8 * h:8 * h + 8] for m in range(TIMES)]
            for m, value in enumerate(differentiate(values)):
                derived[m, v, 8 * h:8 * h + 8] = value
        for peer in peers:
            pltpu.make_async_remote_copy(
                derived.at[pl.ds(2 * peer, 2), pl.ds(v, 1)],
                returned.at[:, pl.ds(v, 1), me // 2, pl.ds(pl.multiple_of(HALF * c, HALF), HALF)],
                back_send, back_recv.at[v],
                device_id={"inst": peer}, device_id_type=MESH,
            ).start()
        for i in range(2):
            returned[i, v, me // 2, pl.ds(pl.multiple_of(HALF * c, HALF), HALF)] = derived[2 * me + i, v]
        return 0

    lax.fori_loop(0, VARS, send_back, 0)

    def finish(v, _):
        part = gathered.at[pl.ds(0, TIMES - 2), pl.ds(v, 1)]
        pltpu.make_async_copy(part, part, back_recv.at[v]).wait()
        pace = freq[0]
        for r in range(LAYERS):
            scaled = pace * step[r]
            for n in range(2):
                fresh[n, v, r] = fresh[n, v, r] - scaled * returned[n, v, r]
        pltpu.make_async_copy(fresh.at[:, pl.ds(v, 1)], out.at[:, pl.ds(v, 1)], store_sem).start()
        return 0

    lax.fori_loop(0, VARS, finish, 0)
    pltpu.make_async_copy(fresh, out, store_sem).wait()
    whole = gathered.at[pl.ds(0, TIMES - 2)]
    pltpu.make_async_copy(whole, whole, out_send).wait()
    pltpu.make_async_copy(whole, whole, back_send).wait()
    layer_copy.wait_send()
    for copy in side_copies:
        copy.wait_send()


def per_device(flow_state, pseudo_step, frequency, flux_jac, donor_offset):
    f32 = jnp.float32
    anywhere = pl.BlockSpec(memory_space=pl.ANY)
    in_hbm = pl.BlockSpec(memory_space=pltpu.HBM)
    dma = pltpu.SemaphoreType.DMA
    return pl.pallas_call(
        kernel,
        name="pseudo_time_step",
        out_shape=jax.ShapeDtypeStruct(flow_state.shape, f32),
        in_specs=[in_hbm] * 5,
        out_specs=anywhere,
        scratch_shapes=[
            pltpu.VMEM((2, VARS, LAYERS + 2, ROWS + 2 * PAD, LANES), f32),
            pltpu.VMEM((LAYERS, ROWS, LANES), f32),
            pltpu.SMEM((1,), f32),
            pltpu.SMEM((3, VARS, VARS), f32),
            pltpu.SMEM((TIMES,), jnp.int32),
            pltpu.VMEM((2, 2, VARS, LAYERS, LANES), f32),
            pltpu.VMEM((2, 2, VARS, LAYERS, LANES), f32),
            pltpu.VMEM((2, 3 * ROWS, LANES), f32),
            pltpu.VMEM((2, ROWS, LANES), f32),
            pltpu.VMEM((TIMES, VARS, HALF, LANES), f32),
            pltpu.VMEM((TIMES, VARS, HALF, LANES), f32),
            pltpu.VMEM((2, VARS, LAYERS, ROWS, LANES), f32),
            pltpu.VMEM((2, VARS, LAYERS, ROWS, LANES), f32),
            dma((6,)), dma, dma((VARS,)), dma, dma((VARS,)), dma((5,)), dma((5,)), dma,
        ],
        compiler_params=pltpu.CompilerParams(
            collective_id=0, has_side_effects=True, vmem_limit_bytes=60 << 20
        ),
        cost_estimate=pl.CostEstimate(flops=40_000_000, bytes_accessed=4_000_000, transcendentals=0),
    )(flow_state, pseudo_step, frequency, flux_jac, donor_offset)


def solution(mesh):
    return jax.shard_map(
        per_device,
        mesh=mesh,
        in_specs=(P("inst", None, "rad", "circ", None), P("rad", "circ", None), P(), P(), P()),
        out_specs=P("inst", None, "rad", "circ", None),
        check_vma=False,
    )
```

```python
import functools

import jax
import jax.numpy as jnp
import numpy as np
from jax import lax
from jax.experimental import pallas as pl
from jax.experimental.pallas import tpu as pltpu
from jax.sharding import PartitionSpec as P

MESH = pl.DeviceIdType.MESH
BEND = (0.3, 0.2, 0.25)
PRODUCE = 0.4
DESTROY = 0.2
VARS = 6
TIMES = 32
LAYERS = 8
ROWS = 32
HALF = 16
LANES = 128
GROUP = 16
PAD = 8


def spectral_weights(length):
    k = np.arange(length)
    sign = np.where(k % 2 == 0, 1.0, -1.0)
    angle = np.pi * np.where(k == 0, 1, k) / length
    weights = 0.5 * sign / np.tan(angle)
    weights[0] = 0.0
    weights[length // 2] = 0.0
    return weights


def circulant(first, rows, fold):
    length = len(first)
    return [
        [first[n - m] if n >= m else fold * first[n - m + length] for m in range(length)]
        for n in range(rows)
    ]


def apply_rows(matrix, values):
    results = []
    for row in matrix:
        total = None
        for weight, value in zip(row, values):
            if abs(weight) < 1e-12:
                continue
            term = np.float32(weight) * value
            total = term if total is None else total + term
        results.append(total)
    return results


def differentiate(values):
    d = spectral_weights(TIMES)
    even = 0.5 * (d[:16] + d[16:])
    odd = 0.5 * (d[:16] - d[16:])
    even_even = 0.5 * (even[:8] + even[8:])
    even_odd = 0.5 * (even[:8] - even[8:])
    sums = [values[m] + values[m + 16] for m in range(16)]
    gaps = [values[m] - values[m + 16] for m in range(16)]
    sum_sums = [sums[m] + sums[m + 8] for m in range(8)]
    sum_gaps = [sums[m] - sums[m + 8] for m in range(8)]
    a = apply_rows(circulant(even_even, 8, 1.0), sum_sums)
    b = apply_rows(circulant(even_odd, 8, -1.0), sum_gaps)
    e = [a[n] + b[n] for n in range(8)] + [a[n] - b[n] for n in range(8)]
    o = apply_rows(circulant(odd, 16, -1.0), gaps)
    return [e[n] + o[n] for n in range(16)] + [e[n] - o[n] for n in range(16)]


def kernel(
    q, dt_hbm, freq, jac_hbm, shift_hbm, out,
    cells, step, jac, shift, rows_out, rows_in, columns, ghosts,
    gathered, derived, returned, fresh,
    local_sem, out_send, out_recv, back_send, back_recv, side_send, side_recv,
):
    me = lax.axis_index("inst")
    rad = lax.axis_index("rad")
    circ = lax.axis_index("circ")
    x, y, c = me // 8, lax.rem(me // 2, 4), lax.rem(me, 2)
    peers = []
    for dx, dy, dc in [
        (1, 2, 0), (1, 2, 1), (1, 1, 0), (1, 3, 0), (1, 1, 1), (1, 3, 1), (1, 0, 0), (1, 0, 1),
        (0, 2, 0), (0, 2, 1), (0, 1, 0), (0, 3, 0), (0, 1, 1), (0, 3, 1), (0, 0, 1),
    ]:
        peers.append((lax.rem(x + dx, 2) * 4 + lax.rem(y + dy, 4)) * 2 + lax.rem(c + dc, 2))
    after = {"circ": lax.rem(circ + 1, 4)}
    before = {"circ": lax.rem(circ + 3, 4)}
    across = {"rad": 1 - rad}

    loads = [
        pltpu.make_async_copy(
            q.at[:, :, r], cells.at[:, :, r + 1, pl.ds(PAD, ROWS)], local_sem.at[0]
        )
        for r in range(LAYERS)
    ]
    for copy in loads:
        copy.start()
    small = [
        pltpu.make_async_copy(dt_hbm, step, local_sem.at[1]),
        pltpu.make_async_copy(jac_hbm, jac, local_sem.at[3]),
        pltpu.make_async_copy(shift_hbm, shift, local_sem.at[4]),
        pltpu.make_async_copy(
            q.at[:, :, me // 2, pl.ds(pl.multiple_of(HALF * c, HALF), HALF)],
            gathered.at[pl.ds(2 * me, 2)], local_sem.at[5],
        ),
    ]
    for copy in small:
        copy.start()

    barrier = pltpu.get_barrier_semaphore()
    for peer in peers:
        pl.semaphore_signal(barrier, inc=1, device_id={"inst": peer}, device_id_type=MESH)
    for peer in (after, before, across):
        pl.semaphore_signal(barrier, inc=1, device_id=peer, device_id_type=MESH)
    pl.semaphore_wait(barrier, GROUP - 1 + 3)

    def send_out(v, _):
        for peer in peers:
            pltpu.make_async_remote_copy(
                q.at[:, pl.ds(v, 1), peer // 2, pl.ds(pl.multiple_of(HALF * lax.rem(peer, 2), HALF), HALF)],
                gathered.at[pl.ds(2 * me, 2), pl.ds(v, 1)],
                out_send, out_recv.at[v],
                device_id={"inst": peer}, device_id_type=MESH,
            ).start()
        return 0

    lax.fori_loop(0, VARS, send_out, 0)
    layer_copy = pltpu.make_async_remote_copy(
        q.at[:, :, (LAYERS - 1) * (1 - rad)],
        cells.at[:, :, (LAYERS + 1) * rad, pl.ds(PAD, ROWS)],
        side_send.at[0], side_recv.at[0], device_id=across, device_id_type=MESH,
    )
    layer_copy.start()

    for copy in loads:
        copy.wait()

    lane = lax.broadcasted_iota(jnp.int32, (ROWS, LANES), 1)

    def pack(n, _):
        packed = jnp.zeros((ROWS, LANES), jnp.float32)
        for v in range(VARS):
            for r in range(LAYERS):
                rows_out[0, n, v, r:r + 1] = cells[n, v, r + 1, PAD + ROWS - 1:PAD + ROWS]
                rows_out[1, n, v, r:r + 1] = cells[n, v, r + 1, PAD:PAD + 1]
                j = v * LAYERS + r
                block = pltpu.roll(cells[n, v, r + 1, PAD:PAD + ROWS], (2 * j - 63) % LANES, 1)
                packed = jnp.where(lane // 2 == j, block, packed)
        columns[n, ROWS:2 * ROWS] = packed
        return 0

    lax.fori_loop(0, 2, pack, 0)
    side_copies = [
        pltpu.make_async_remote_copy(
            rows_out.at[0], rows_in.at[0], side_send.at[1], side_recv.at[1],
            device_id=after, device_id_type=MESH,
        ),
        pltpu.make_async_remote_copy(
            rows_out.at[1], rows_in.at[1], side_send.at[2], side_recv.at[2],
            device_id=before, device_id_type=MESH,
        ),
        pltpu.make_async_remote_copy(
            columns.at[:, pl.ds(ROWS, ROWS)], columns.at[:, pl.ds(0, ROWS)],
            side_send.at[3], side_recv.at[3], device_id=after, device_id_type=MESH,
        ),
        pltpu.make_async_remote_copy(
            columns.at[:, pl.ds(ROWS, ROWS)], columns.at[:, pl.ds(2 * ROWS, ROWS)],
            side_send.at[4], side_recv.at[4], device_id=before, device_id_type=MESH,
        ),
    ]
    for copy in side_copies:
        copy.start()
    cells[:, :, (LAYERS + 1) * rad, PAD:PAD + ROWS] = jnp.zeros((2, VARS, ROWS, LANES), jnp.float32)
    for copy in small:
        copy.wait()

    def send_back(v, _):
        part = gathered.at[pl.ds(0, TIMES - 2), pl.ds(v, 1)]
        pltpu.make_async_copy(part, part, out_recv.at[v]).wait()
        for h in range(HALF // 8):
            values = [gathered[m, v, 8 * h:8 * h + 8] for m in range(TIMES)]
            for m, value in enumerate(differentiate(values)):
                derived[m, v, 8 * h:8 * h + 8] = value
        for peer in peers:
            pltpu.make_async_remote_copy(
                derived.at[pl.ds(2 * peer, 2), pl.ds(v, 1)],
                returned.at[:, pl.ds(v, 1), me // 2, pl.ds(pl.multiple_of(HALF * c, HALF), HALF)],
                back_send, back_recv.at[v],
                device_id={"inst": peer}, device_id_type=MESH,
            ).start()
        for i in range(2):
            returned[i, v, me // 2, pl.ds(pl.multiple_of(HALF * c, HALF), HALF)] = derived[2 * me + i, v]
        return 0

    lax.fori_loop(0, VARS, send_back, 0)

    for copy in side_copies:
        copy.wait_recv()

    def unpack(n, _):
        for v in range(VARS):
            for r in range(LAYERS):
                cells[n, v, r + 1, PAD - 1:PAD] = rows_in[0, n, v, r:r + 1]
                cells[n, v, r + 1, PAD + ROWS:PAD + ROWS + 1] = rows_in[1, n, v, r:r + 1]
        s = shift[2 * me + n]
        stator = columns[n, pl.ds(ROWS + s, ROWS)]
        rotor = columns[n, pl.ds(ROWS - s, ROWS)]
        ghosts[n] = jnp.where(lane % 2 == 0, pltpu.roll(rotor, LANES - 1, 1), pltpu.roll(stator, 1, 1))
        return 0

    lax.fori_loop(0, 2, unpack, 0)
    layer_copy.wait_recv()

    def spatial(t, _):
        n, r = t // LAYERS, lax.rem(t, LAYERS)
        ghost = ghosts[n]
        here, sides = [], [[], [], []]
        for v in range(VARS):
            now = cells[n, v, r + 1, PAD:PAD + ROWS]
            here.append(now)
            sides[0].append((cells[n, v, r, PAD:PAD + ROWS], cells[n, v, r + 2, PAD:PAD + ROWS]))
            sides[1].append((cells[n, v, r + 1, PAD - 1:PAD + ROWS - 1], cells[n, v, r + 1, PAD + 1:PAD + ROWS + 1]))
            first = 63 - 2 * LAYERS * v
            placed = pltpu.roll(ghost, (first if first > 2 * LAYERS - 2 else first + LANES) - 2 * r, 1)
            lower = jnp.where(lane == 64, placed, jnp.where(lane == 0, 0.0, pltpu.roll(now, 1, 1)))
            upper = jnp.where(lane == 63, placed, jnp.where(lane == LANES - 1, 0.0, pltpu.roll(now, LANES - 1, 1)))
            sides[2].append((lower, upper))
        linear = [None] * VARS
        rest = [3.0 * now for now in here]
        for d in range(3):
            low0 = (0.25 * BEND[d]) * sides[d][0][0] + 0.5
            high0 = (0.25 * BEND[d]) * sides[d][0][1] - 0.5
            for v in range(VARS):
                low, high = sides[d][v]
                rest[v] = rest[v] + (high * high0 - low * low0)
                gap = high - low
                for u in range(VARS):
                    term = jac[d, u, v] * gap
                    linear[u] = term if linear[u] is None else linear[u] + term
        eddy = here[5]
        source = PRODUCE * eddy * jnp.sqrt(1.0 + here[1] * here[1] + here[2] * here[2]) - DESTROY * eddy * jnp.abs(eddy)
        rest[5] = rest[5] - source
        pace = step[r]
        for v in range(VARS):
            fresh[n, v, r] = here[v] - pace * (rest[v] + 0.5 * linear[v])
        return 0

    lax.fori_loop(0, 2 * LAYERS, spatial, 0)

    def finish(v, _):
        part = gathered.at[pl.ds(0, TIMES - 2), pl.ds(v, 1)]
        pltpu.make_async_copy(part, part, back_recv.at[v]).wait()
        pace = freq[0]
        for r in range(LAYERS):
            scaled = pace * step[r]
            for n in range(2):
                out[n, v, r] = fresh[n, v, r] - scaled * returned[n, v, r]
        return 0

    lax.fori_loop(0, VARS, finish, 0)
    whole = gathered.at[pl.ds(0, TIMES - 2)]
    pltpu.make_async_copy(whole, whole, out_send).wait()
    pltpu.make_async_copy(whole, whole, back_send).wait()
    layer_copy.wait_send()
    for copy in side_copies:
        copy.wait_send()


def per_device(flow_state, pseudo_step, frequency, flux_jac, donor_offset):
    f32 = jnp.float32
    anywhere = pl.BlockSpec(memory_space=pl.ANY)
    scalar = pl.BlockSpec(memory_space=pltpu.SMEM)
    hbm = functools.partial(pltpu.with_memory_space_constraint, memory_space=pltpu.HBM)
    dma = pltpu.SemaphoreType.DMA
    return pl.pallas_call(
        kernel,
        name="pseudo_time_step",
        out_shape=pltpu.VMEM(flow_state.shape, f32),
        in_specs=[anywhere, anywhere, scalar, anywhere, anywhere],
        out_specs=pl.BlockSpec(memory_space=pltpu.VMEM),
        scratch_shapes=[
            pltpu.VMEM((2, VARS, LAYERS + 2, ROWS + 2 * PAD, LANES), f32),
            pltpu.VMEM((LAYERS, ROWS, LANES), f32),
            pltpu.SMEM((3, VARS, VARS), f32),
            pltpu.SMEM((TIMES,), jnp.int32),
            pltpu.VMEM((2, 2, VARS, LAYERS, LANES), f32),
            pltpu.VMEM((2, 2, VARS, LAYERS, LANES), f32),
            pltpu.VMEM((2, 3 * ROWS, LANES), f32),
            pltpu.VMEM((2, ROWS, LANES), f32),
            pltpu.VMEM((TIMES, VARS, HALF, LANES), f32),
            pltpu.VMEM((TIMES, VARS, HALF, LANES), f32),
            pltpu.VMEM((2, VARS, LAYERS, ROWS, LANES), f32),
            pltpu.VMEM((2, VARS, LAYERS, ROWS, LANES), f32),
            dma((6,)), dma, dma((VARS,)), dma, dma((VARS,)), dma((5,)), dma((5,)),
        ],
        compiler_params=pltpu.CompilerParams(
            collective_id=0, has_side_effects=True, vmem_limit_bytes=40 << 20
        ),
        cost_estimate=pl.CostEstimate(flops=40_000_000, bytes_accessed=4_000_000, transcendentals=0),
    )(hbm(flow_state), hbm(pseudo_step), frequency, hbm(flux_jac), hbm(donor_offset))


def solution(mesh):
    return jax.shard_map(
        per_device,
        mesh=mesh,
        in_specs=(P("inst", None, "rad", "circ", None), P("rad", "circ", None), P(), P(), P()),
        out_specs=P("inst", None, "rad", "circ", None),
        check_vma=False,
    )
```

```python
import functools

import jax
import jax.numpy as jnp
import numpy as np
from jax import lax
from jax.experimental import pallas as pl
from jax.experimental.pallas import tpu as pltpu
from jax.sharding import PartitionSpec as P

MESH = pl.DeviceIdType.MESH
BEND = (0.3, 0.2, 0.25)
PRODUCE = 0.4
DESTROY = 0.2
VARS = 6
TIMES = 32
LAYERS = 8
ROWS = 32
TILE = 8
TAKE = 2
GROUPS = VARS // TAKE
LANES = 128
GROUP = 16
PAD = 8


def spectral_weights(length):
    k = np.arange(length)
    sign = np.where(k % 2 == 0, 1.0, -1.0)
    angle = np.pi * np.where(k == 0, 1, k) / length
    weights = 0.5 * sign / np.tan(angle)
    weights[0] = 0.0
    weights[length // 2] = 0.0
    return weights


def circulant(first, rows, fold):
    length = len(first)
    return [
        [first[n - m] if n >= m else fold * first[n - m + length] for m in range(length)]
        for n in range(rows)
    ]


def apply_rows(matrix, values):
    results = []
    for row in matrix:
        total = None
        for weight, value in zip(row, values):
            if abs(weight) < 1e-12:
                continue
            term = np.float32(weight) * value
            total = term if total is None else total + term
        results.append(total)
    return results


def differentiate(values):
    d = spectral_weights(TIMES)
    even = 0.5 * (d[:16] + d[16:])
    odd = 0.5 * (d[:16] - d[16:])
    even_even = 0.5 * (even[:8] + even[8:])
    even_odd = 0.5 * (even[:8] - even[8:])
    sums = [values[m] + values[m + 16] for m in range(16)]
    gaps = [values[m] - values[m + 16] for m in range(16)]
    sum_sums = [sums[m] + sums[m + 8] for m in range(8)]
    sum_gaps = [sums[m] - sums[m + 8] for m in range(8)]
    a = apply_rows(circulant(even_even, 8, 1.0), sum_sums)
    b = apply_rows(circulant(even_odd, 8, -1.0), sum_gaps)
    e = [a[n] + b[n] for n in range(8)] + [a[n] - b[n] for n in range(8)]
    o = apply_rows(circulant(odd, 16, -1.0), gaps)
    return [e[n] + o[n] for n in range(16)] + [e[n] - o[n] for n in range(16)]


def kernel(
    q, dt_hbm, freq, jac_hbm, shift_hbm, out,
    cells, step, jac, shift, rows_out, rows_in, columns, ghosts,
    gathered, beyond, derived, returned, fresh,
    local_sem, out_send, out_recv, back_send, back_recv, side_send, side_recv, swap_send, swap_recv,
):
    me = lax.axis_index("inst")
    rad = lax.axis_index("rad")
    circ = lax.axis_index("circ")
    x, y, c = me // 8, lax.rem(me // 2, 4), lax.rem(me, 2)
    peers = []
    for dx, dy, dc in [
        (1, 2, 0), (1, 2, 1), (1, 1, 0), (1, 3, 0), (1, 1, 1), (1, 3, 1), (1, 0, 0), (1, 0, 1),
        (0, 2, 0), (0, 2, 1), (0, 1, 0), (0, 3, 0), (0, 1, 1), (0, 3, 1), (0, 0, 1),
    ]:
        px, py, pc = lax.rem(x + dx, 2), lax.rem(y + dy, 4), lax.rem(c + dc, 2)
        peers.append(((px * 4 + py) * 2 + pc, px * 4 + pc * 2, pl.multiple_of(py * TILE, TILE)))
    after = {"circ": lax.rem(circ + 1, 4)}
    before = {"circ": lax.rem(circ + 3, 4)}
    across = {"rad": 1 - rad, "inst": ((1 - x) * 4 + y) * 2 + 1 - c}
    meets = jnp.logical_and(x == 1 - rad, c == 1 - rad)

    barrier = pltpu.get_barrier_semaphore()
    for peer, _, _ in peers:
        pl.semaphore_signal(barrier, inc=1, device_id={"inst": peer}, device_id_type=MESH)
    for peer in (after, before, across):
        pl.semaphore_signal(barrier, inc=1, device_id=peer, device_id_type=MESH)

    my_layer, my_row = x * 4 + c * 2, pl.multiple_of(y * TILE, TILE)
    loads = [
        pltpu.make_async_copy(
            q.at[:, :, r], cells.at[:, :, r + 1, pl.ds(PAD, ROWS)], local_sem.at[0]
        )
        for r in range(LAYERS)
    ]
    for copy in loads:
        copy.start()
    small = [
        pltpu.make_async_copy(dt_hbm, step, local_sem.at[1]),
        pltpu.make_async_copy(jac_hbm, jac, local_sem.at[2]),
        pltpu.make_async_copy(shift_hbm, shift, local_sem.at[3]),
    ]
    for slot in range(2):
        small.append(
            pltpu.make_async_copy(
                q.at[:, :, my_layer + lax.rem(slot + 1 - rad, 2), pl.ds(my_row, TILE)],
                gathered.at[slot, pl.ds(2 * me, 2)], local_sem.at[4 + slot],
            )
        )
    for copy in small:
        copy.start()
    pl.semaphore_wait(barrier, GROUP - 1 + 3)

    def send_out(k, _):
        slot, g = k // GROUPS, lax.rem(k, GROUPS)
        for peer, layer, row in peers:
            pltpu.make_async_remote_copy(
                q.at[:, pl.ds(g * TAKE, TAKE), layer + lax.rem(slot + 1 - rad, 2), pl.ds(row, TILE)],
                gathered.at[slot, pl.ds(2 * me, 2), pl.ds(g * TAKE, TAKE)],
                out_send, out_recv.at[k],
                device_id={"inst": peer}, device_id_type=MESH,
            ).start()
        return 0

    lax.fori_loop(0, 2 * GROUPS, send_out, 0)

    for copy in loads:
        copy.wait()

    lane = lax.broadcasted_iota(jnp.int32, (ROWS, LANES), 1)

    def pack(n, _):
        packed = jnp.zeros((ROWS, LANES), jnp.float32)
        for v in range(VARS):
            for r in range(LAYERS):
                rows_out[0, n, v, r:r + 1] = cells[n, v, r + 1, PAD + ROWS - 1:PAD + ROWS]
                rows_out[1, n, v, r:r + 1] = cells[n, v, r + 1, PAD:PAD + 1]
                j = v * LAYERS + r
                block = pltpu.roll(cells[n, v, r + 1, PAD:PAD + ROWS], (2 * j - 63) % LANES, 1)
                packed = jnp.where(lane // 2 == j, block, packed)
        columns[n, ROWS:2 * ROWS] = packed
        return 0

    lax.fori_loop(0, 2, pack, 0)
    side_copies = [
        pltpu.make_async_remote_copy(
            rows_out.at[0], rows_in.at[0], side_send.at[0], side_recv.at[0],
            device_id=after, device_id_type=MESH,
        ),
        pltpu.make_async_remote_copy(
            rows_out.at[1], rows_in.at[1], side_send.at[1], side_recv.at[1],
            device_id=before, device_id_type=MESH,
        ),
        pltpu.make_async_remote_copy(
            columns.at[:, pl.ds(ROWS, ROWS)], columns.at[:, pl.ds(0, ROWS)],
            side_send.at[2], side_recv.at[2], device_id=after, device_id_type=MESH,
        ),
        pltpu.make_async_remote_copy(
            columns.at[:, pl.ds(ROWS, ROWS)], columns.at[:, pl.ds(2 * ROWS, ROWS)],
            side_send.at[3], side_recv.at[3], device_id=before, device_id_type=MESH,
        ),
    ]
    for copy in side_copies:
        copy.start()
    cells[:, :, 0, PAD:PAD + ROWS] = jnp.zeros((2, VARS, ROWS, LANES), jnp.float32)
    cells[:, :, LAYERS + 1, PAD:PAD + ROWS] = jnp.zeros((2, VARS, ROWS, LANES), jnp.float32)
    for copy in small:
        copy.wait()

    def wait_part(sem):
        part = gathered.at[0, pl.ds(0, TIMES - 2), pl.ds(0, TAKE)]
        pltpu.make_async_copy(part, part, sem).wait()

    swaps = [
        pltpu.make_async_remote_copy(
            gathered.at[0, :, pl.ds(g * TAKE, TAKE)], beyond.at[:, pl.ds(g * TAKE, TAKE)],
            swap_send.at[g], swap_recv.at[g], device_id=across, device_id_type=MESH,
        )
        for g in range(GROUPS)
    ]

    @pl.when(meets)
    def _():
        for g in range(GROUPS):
            wait_part(out_recv.at[g])
            swaps[g].start()

    pace = freq[0]
    side = (1 - 2 * rad).astype(jnp.float32)

    def radial_term(m, _):
        w = [beyond[m, v] for v in range(VARS)]
        curved = (0.25 * BEND[0]) * w[0]
        for u in range(VARS):
            total = curved * w[u]
            for v in range(VARS):
                total = total + (0.5 * jac[0, u, v]) * w[v]
            beyond[m, u] = side * total - 0.5 * w[u]
        return 0

    def send_back(k, _):
        slot = lax.rem(k // GROUPS + meets.astype(jnp.int32), 2)
        g = lax.rem(k, GROUPS)
        meeting = jnp.logical_and(meets, slot == 0)

        @pl.when(jnp.logical_not(meeting))
        def _():
            wait_part(out_recv.at[slot * GROUPS + g])

        @pl.when(jnp.logical_and(meeting, g == 0))
        def _():
            for swap in swaps:
                swap.wait_recv()
            lax.fori_loop(0, TIMES, radial_term, 0)

        for i in range(TAKE):
            v = g * TAKE + i
            values = [gathered[slot, m, v] for m in range(TIMES)]
            for m, value in enumerate(differentiate(values)):
                derived[slot, m, v] = pace * value

        @pl.when(meeting)
        def _():
            for i in range(TAKE):
                v = g * TAKE + i
                for m in range(TIMES):
                    derived[0, m, v] = derived[0, m, v] + beyond[m, v]

        layer = my_layer + lax.rem(slot + 1 - rad, 2)
        for peer, _, _ in peers:
            pltpu.make_async_remote_copy(
                derived.at[slot, pl.ds(2 * peer, 2), pl.ds(g * TAKE, TAKE)],
                returned.at[:, pl.ds(g * TAKE, TAKE), layer, pl.ds(my_row, TILE)],
                back_send, back_recv.at[slot * GROUPS + g],
                device_id={"inst": peer}, device_id_type=MESH,
            ).start()
        for n in range(2):
            for i in range(TAKE):
                v = g * TAKE + i
                returned[n, v, layer, pl.ds(my_row, TILE)] = derived[slot, 2 * me + n, v]
        return 0

    lax.fori_loop(0, 2 * GROUPS, send_back, 0)

    for copy in side_copies:
        copy.wait_recv()

    def unpack(n, _):
        for v in range(VARS):
            for r in range(LAYERS):
                cells[n, v, r + 1, PAD - 1:PAD] = rows_in[0, n, v, r:r + 1]
                cells[n, v, r + 1, PAD + ROWS:PAD + ROWS + 1] = rows_in[1, n, v, r:r + 1]
        s = shift[2 * me + n]
        stator = columns[n, pl.ds(ROWS + s, ROWS)]
        rotor = columns[n, pl.ds(ROWS - s, ROWS)]
        ghosts[n] = jnp.where(lane % 2 == 0, pltpu.roll(rotor, LANES - 1, 1), pltpu.roll(stator, 1, 1))
        return 0

    lax.fori_loop(0, 2, unpack, 0)

    def spatial(t, _):
        n, r = t // LAYERS, lax.rem(t, LAYERS)
        ghost = ghosts[n]
        here, sides = [], [[], [], []]
        for v in range(VARS):
            now = cells[n, v, r + 1, PAD:PAD + ROWS]
            here.append(now)
            sides[0].append((cells[n, v, r, PAD:PAD + ROWS], cells[n, v, r + 2, PAD:PAD + ROWS]))
            sides[1].append((cells[n, v, r + 1, PAD - 1:PAD + ROWS - 1], cells[n, v, r + 1, PAD + 1:PAD + ROWS + 1]))
            first = 63 - 2 * LAYERS * v
            placed = pltpu.roll(ghost, (first if first > 2 * LAYERS - 2 else first + LANES) - 2 * r, 1)
            lower = jnp.where(lane == 64, placed, jnp.where(lane == 0, 0.0, pltpu.roll(now, 1, 1)))
            upper = jnp.where(lane == 63, placed, jnp.where(lane == LANES - 1, 0.0, pltpu.roll(now, LANES - 1, 1)))
            sides[2].append((lower, upper))
        linear = [None] * VARS
        rest = [3.0 * now for now in here]
        for d in range(3):
            low0 = (0.25 * BEND[d]) * sides[d][0][0] + 0.5
            high0 = (0.25 * BEND[d]) * sides[d][0][1] - 0.5
            for v in range(VARS):
                low, high = sides[d][v]
                rest[v] = rest[v] + (high * high0 - low * low0)
                gap = high - low
                for u in range(VARS):
                    term = jac[d, u, v] * gap
                    linear[u] = term if linear[u] is None else linear[u] + term
        eddy = here[5]
        source = PRODUCE * eddy * jnp.sqrt(1.0 + here[1] * here[1] + here[2] * here[2]) - DESTROY * eddy * jnp.abs(eddy)
        rest[5] = rest[5] - source
        pace = step[r]
        for v in range(VARS):
            fresh[n, v, r] = here[v] - pace * (rest[v] + 0.5 * linear[v])
        return 0

    lax.fori_loop(0, 2 * LAYERS, spatial, 0)

    def finish(k, _):
        slot, g = 1 - k // GROUPS, lax.rem(k, GROUPS)
        wait_part(back_recv.at[slot * GROUPS + g])
        for pair in range(LAYERS // 2):
            r = 2 * pair + lax.rem(slot + 1 - rad, 2)
            scaled = step[r]
            for n in range(2):
                for i in range(TAKE):
                    v = g * TAKE + i
                    out[n, v, r] = fresh[n, v, r] - scaled * returned[n, v, r]
        return 0

    lax.fori_loop(0, 2 * GROUPS, finish, 0)
    whole = gathered.at[:, pl.ds(0, TIMES - 2)]
    pltpu.make_async_copy(whole, whole, out_send).wait()
    pltpu.make_async_copy(whole, whole, back_send).wait()
    for copy in side_copies:
        copy.wait_send()

    @pl.when(meets)
    def _():
        for swap in swaps:
            swap.wait_send()


def per_device(flow_state, pseudo_step, frequency, flux_jac, donor_offset):
    f32 = jnp.float32
    anywhere = pl.BlockSpec(memory_space=pl.ANY)
    scalar = pl.BlockSpec(memory_space=pltpu.SMEM)
    hbm = functools.partial(pltpu.with_memory_space_constraint, memory_space=pltpu.HBM)
    dma = pltpu.SemaphoreType.DMA
    return pl.pallas_call(
        kernel,
        name="pseudo_time_step",
        out_shape=pltpu.VMEM(flow_state.shape, f32),
        in_specs=[anywhere, anywhere, scalar, anywhere, anywhere],
        out_specs=pl.BlockSpec(memory_space=pltpu.VMEM),
        scratch_shapes=[
            pltpu.VMEM((2, VARS, LAYERS + 2, ROWS + 2 * PAD, LANES), f32),
            pltpu.VMEM((LAYERS, ROWS, LANES), f32),
            pltpu.SMEM((3, VARS, VARS), f32),
            pltpu.SMEM((TIMES,), jnp.int32),
            pltpu.VMEM((2, 2, VARS, LAYERS, LANES), f32),
            pltpu.VMEM((2, 2, VARS, LAYERS, LANES), f32),
            pltpu.VMEM((2, 3 * ROWS, LANES), f32),
            pltpu.VMEM((2, ROWS, LANES), f32),
            pltpu.VMEM((2, TIMES, VARS, TILE, LANES), f32),
            pltpu.VMEM((TIMES, VARS, TILE, LANES), f32),
            pltpu.VMEM((2, TIMES, VARS, TILE, LANES), f32),
            pltpu.VMEM((2, VARS, LAYERS, ROWS, LANES), f32),
            pltpu.VMEM((2, VARS, LAYERS, ROWS, LANES), f32),
            dma((6,)), dma, dma((2 * GROUPS,)), dma, dma((2 * GROUPS,)),
            dma((4,)), dma((4,)), dma((GROUPS,)), dma((GROUPS,)),
        ],
        compiler_params=pltpu.CompilerParams(
            collective_id=0, has_side_effects=True, vmem_limit_bytes=40 << 20
        ),
        cost_estimate=pl.CostEstimate(flops=40_000_000, bytes_accessed=4_000_000, transcendentals=0),
    )(hbm(flow_state), hbm(pseudo_step), frequency, hbm(flux_jac), hbm(donor_offset))


def solution(mesh):
    return jax.shard_map(
        per_device,
        mesh=mesh,
        in_specs=(P("inst", None, "rad", "circ", None), P("rad", "circ", None), P(), P(), P()),
        out_specs=P("inst", None, "rad", "circ", None),
        check_vma=False,
    )
```

```python
import functools

import jax
import jax.numpy as jnp
import numpy as np
from jax import lax
from jax.experimental import pallas as pl
from jax.experimental.pallas import tpu as pltpu
from jax.sharding import PartitionSpec as P

MESH = pl.DeviceIdType.MESH
BEND = (0.3, 0.2, 0.25)
PRODUCE = 0.4
DESTROY = 0.2
VARS = 6
TIMES = 32
LAYERS = 8
ROWS = 32
TILE = 8
TAKE = 3
GROUPS = VARS // TAKE
LANES = 128
GROUP = 16
PAD = 8


def spectral_weights(length):
    k = np.arange(length)
    sign = np.where(k % 2 == 0, 1.0, -1.0)
    angle = np.pi * np.where(k == 0, 1, k) / length
    weights = 0.5 * sign / np.tan(angle)
    weights[0] = 0.0
    weights[length // 2] = 0.0
    return weights


def circulant(first, rows, fold):
    length = len(first)
    return [
        [first[n - m] if n >= m else fold * first[n - m + length] for m in range(length)]
        for n in range(rows)
    ]


def apply_rows(matrix, values):
    results = []
    for row in matrix:
        total = None
        for weight, value in zip(row, values):
            if abs(weight) < 1e-12:
                continue
            term = np.float32(weight) * value
            total = term if total is None else total + term
        results.append(total)
    return results


def differentiate(values):
    d = spectral_weights(TIMES)
    even = 0.5 * (d[:16] + d[16:])
    odd = 0.5 * (d[:16] - d[16:])
    even_even = 0.5 * (even[:8] + even[8:])
    even_odd = 0.5 * (even[:8] - even[8:])
    sums = [values[m] + values[m + 16] for m in range(16)]
    gaps = [values[m] - values[m + 16] for m in range(16)]
    sum_sums = [sums[m] + sums[m + 8] for m in range(8)]
    sum_gaps = [sums[m] - sums[m + 8] for m in range(8)]
    a = apply_rows(circulant(even_even, 8, 1.0), sum_sums)
    b = apply_rows(circulant(even_odd, 8, -1.0), sum_gaps)
    e = [a[n] + b[n] for n in range(8)] + [a[n] - b[n] for n in range(8)]
    o = apply_rows(circulant(odd, 16, -1.0), gaps)
    return [e[n] + o[n] for n in range(16)] + [e[n] - o[n] for n in range(16)]


def kernel(
    q, dt_hbm, freq, jac_hbm, shift_hbm, out,
    cells, step, jac, shift, rows_out, rows_in, columns, ghosts,
    gathered, beyond, derived, returned, fresh,
    local_sem, out_send, out_recv, back_send, back_recv, side_send, side_recv, swap_send, swap_recv, entered,
):
    me = lax.axis_index("inst")
    rad = lax.axis_index("rad")
    circ = lax.axis_index("circ")
    x, y, c = me // 8, lax.rem(me // 2, 4), lax.rem(me, 2)
    peers = []
    for dx, dy, dc in [
        (1, 2, 0), (1, 2, 1), (1, 1, 0), (1, 3, 0), (1, 1, 1), (1, 3, 1), (1, 0, 0), (1, 0, 1),
        (0, 2, 0), (0, 2, 1), (0, 1, 0), (0, 3, 0), (0, 1, 1), (0, 3, 1), (0, 0, 1),
    ]:
        px, py, pc = lax.rem(x + dx, 2), lax.rem(y + dy, 4), lax.rem(c + dc, 2)
        peers.append(((px * 4 + py) * 2 + pc, px * 4 + pc * 2, pl.multiple_of(py * TILE, TILE)))
    after = {"circ": lax.rem(circ + 1, 4)}
    before = {"circ": lax.rem(circ + 3, 4)}
    across = {"rad": 1 - rad, "inst": ((1 - x) * 4 + y) * 2 + 1 - c}
    meets = jnp.logical_and(x == 1 - rad, c == 1 - rad)

    barrier = pltpu.get_barrier_semaphore()
    for dx, dy in [(1, 2), (1, 1), (1, 3), (0, 2), (1, 0), (0, 1), (0, 3)]:
        chip = lax.rem(x + dx, 2) * 4 + lax.rem(y + dy, 4)
        pl.semaphore_signal(barrier, inc=1, device_id={"inst": 2 * chip}, device_id_type=MESH)

    @pl.when(c == 1)
    def _():
        pl.semaphore_signal(barrier, inc=1, device_id={"inst": me - c}, device_id_type=MESH)

    for axis, place, chip in (
        ("circ", after["circ"], me // 2),
        ("circ", before["circ"], me // 2),
        ("rad", 1 - rad, (1 - x) * 4 + y),
    ):
        pl.semaphore_signal(
            barrier, inc=1, device_id={axis: place, "inst": 2 * chip + 1}, device_id_type=MESH
        )

    my_layer, my_row = x * 4 + c * 2, pl.multiple_of(y * TILE, TILE)
    loads = [
        pltpu.make_async_copy(
            q.at[:, :, r], cells.at[:, :, r + 1, pl.ds(PAD, ROWS)], local_sem.at[0]
        )
        for r in range(LAYERS)
    ]
    for copy in loads:
        copy.start()
    small = [
        pltpu.make_async_copy(dt_hbm, step, local_sem.at[1]),
        pltpu.make_async_copy(jac_hbm, jac, local_sem.at[2]),
        pltpu.make_async_copy(shift_hbm, shift, local_sem.at[3]),
    ]
    for slot in range(2):
        small.append(
            pltpu.make_async_copy(
                q.at[:, :, my_layer + lax.rem(slot + 1 - rad, 2), pl.ds(my_row, TILE)],
                gathered.at[slot, pl.ds(2 * me, 2)], local_sem.at[4 + slot],
            )
        )
    for copy in small:
        copy.start()

    @pl.when(c == 0)
    def _():
        pl.semaphore_wait(barrier, GROUP - 1)
        pl.semaphore_signal(entered, inc=1, device_id={"inst": me + 1 - c}, device_id_type=MESH)

    @pl.when(c == 1)
    def _():
        pl.semaphore_wait(entered, 1)

    def send_out(k, _):
        slot, g = k // GROUPS, lax.rem(k, GROUPS)
        for peer, layer, row in peers:
            pltpu.make_async_remote_copy(
                q.at[:, pl.ds(g * TAKE, TAKE), layer + lax.rem(slot + 1 - rad, 2), pl.ds(row, TILE)],
                gathered.at[slot, pl.ds(2 * me, 2), pl.ds(g * TAKE, TAKE)],
                out_send, out_recv.at[k],
                device_id={"inst": peer}, device_id_type=MESH,
            ).start()
        return 0

    lax.fori_loop(0, 2 * GROUPS, send_out, 0)

    for copy in loads:
        copy.wait()

    lane = lax.broadcasted_iota(jnp.int32, (ROWS, LANES), 1)

    def pack(n, _):
        packed = jnp.zeros((ROWS, LANES), jnp.float32)
        for v in range(VARS):
            for r in range(LAYERS):
                rows_out[0, n, v, r:r + 1] = cells[n, v, r + 1, PAD + ROWS - 1:PAD + ROWS]
                rows_out[1, n, v, r:r + 1] = cells[n, v, r + 1, PAD:PAD + 1]
                j = v * LAYERS + r
                block = pltpu.roll(cells[n, v, r + 1, PAD:PAD + ROWS], (2 * j - 63) % LANES, 1)
                packed = jnp.where(lane // 2 == j, block, packed)
        columns[n, ROWS:2 * ROWS] = packed
        return 0

    lax.fori_loop(0, 2, pack, 0)
    side_copies = [
        pltpu.make_async_remote_copy(
            rows_out.at[0], rows_in.at[0], side_send.at[0], side_recv.at[0],
            device_id=after, device_id_type=MESH,
        ),
        pltpu.make_async_remote_copy(
            rows_out.at[1], rows_in.at[1], side_send.at[1], side_recv.at[1],
            device_id=before, device_id_type=MESH,
        ),
        pltpu.make_async_remote_copy(
            columns.at[:, pl.ds(ROWS, ROWS)], columns.at[:, pl.ds(0, ROWS)],
            side_send.at[2], side_recv.at[2], device_id=after, device_id_type=MESH,
        ),
        pltpu.make_async_remote_copy(
            columns.at[:, pl.ds(ROWS, ROWS)], columns.at[:, pl.ds(2 * ROWS, ROWS)],
            side_send.at[3], side_recv.at[3], device_id=before, device_id_type=MESH,
        ),
    ]

    @pl.when(c == 1)
    def _():
        pl.semaphore_wait(barrier, 6)
        pl.semaphore_signal(entered, inc=1, device_id={"inst": me - c}, device_id_type=MESH)

    @pl.when(c == 0)
    def _():
        pl.semaphore_wait(entered, 1)

    for copy in side_copies:
        copy.start()
    cells[:, :, 0, PAD:PAD + ROWS] = jnp.zeros((2, VARS, ROWS, LANES), jnp.float32)
    cells[:, :, LAYERS + 1, PAD:PAD + ROWS] = jnp.zeros((2, VARS, ROWS, LANES), jnp.float32)
    for copy in small:
        copy.wait()

    def wait_part(sem):
        part = gathered.at[0, pl.ds(0, TIMES - 2), pl.ds(0, TAKE)]
        pltpu.make_async_copy(part, part, sem).wait()

    swaps = [
        pltpu.make_async_remote_copy(
            gathered.at[0, :, pl.ds(g * TAKE, TAKE)], beyond.at[:, pl.ds(g * TAKE, TAKE)],
            swap_send.at[g], swap_recv.at[g], device_id=across, device_id_type=MESH,
        )
        for g in range(GROUPS)
    ]

    @pl.when(meets)
    def _():
        for g in range(GROUPS):
            wait_part(out_recv.at[g])
            swaps[g].start()

    pace = freq[0]
    side = (1 - 2 * rad).astype(jnp.float32)

    def radial_term(m, _):
        w = [beyond[m, v] for v in range(VARS)]
        curved = (0.25 * BEND[0]) * w[0]
        for u in range(VARS):
            total = curved * w[u]
            for v in range(VARS):
                total = total + (0.5 * jac[0, u, v]) * w[v]
            beyond[m, u] = side * total - 0.5 * w[u]
        return 0

    def send_back(k, _):
        slot = lax.rem(k // GROUPS + meets.astype(jnp.int32), 2)
        g = lax.rem(k, GROUPS)
        meeting = jnp.logical_and(meets, slot == 0)

        @pl.when(jnp.logical_not(meeting))
        def _():
            wait_part(out_recv.at[slot * GROUPS + g])

        @pl.when(jnp.logical_and(meeting, g == 0))
        def _():
            for swap in swaps:
                swap.wait_recv()
            lax.fori_loop(0, TIMES, radial_term, 0)

        for i in range(TAKE):
            v = g * TAKE + i
            values = [gathered[slot, m, v] for m in range(TIMES)]
            for m, value in enumerate(differentiate(values)):
                derived[slot, m, v] = pace * value

        @pl.when(meeting)
        def _():
            for i in range(TAKE):
                v = g * TAKE + i
                for m in range(TIMES):
                    derived[0, m, v] = derived[0, m, v] + beyond[m, v]

        layer = my_layer + lax.rem(slot + 1 - rad, 2)
        for peer, _, _ in peers:
            pltpu.make_async_remote_copy(
                derived.at[slot, pl.ds(2 * peer, 2), pl.ds(g * TAKE, TAKE)],
                returned.at[:, pl.ds(g * TAKE, TAKE), layer, pl.ds(my_row, TILE)],
                back_send, back_recv.at[slot * GROUPS + g],
                device_id={"inst": peer}, device_id_type=MESH,
            ).start()
        for n in range(2):
            for i in range(TAKE):
                v = g * TAKE + i
                returned[n, v, layer, pl.ds(my_row, TILE)] = derived[slot, 2 * me + n, v]
        return 0

    lax.fori_loop(0, 2 * GROUPS, send_back, 0)

    for copy in side_copies:
        copy.wait_recv()

    def unpack(n, _):
        for v in range(VARS):
            for r in range(LAYERS):
                cells[n, v, r + 1, PAD - 1:PAD] = rows_in[0, n, v, r:r + 1]
                cells[n, v, r + 1, PAD + ROWS:PAD + ROWS + 1] = rows_in[1, n, v, r:r + 1]
        s = shift[2 * me + n]
        stator = columns[n, pl.ds(ROWS + s, ROWS)]
        rotor = columns[n, pl.ds(ROWS - s, ROWS)]
        ghosts[n] = jnp.where(lane % 2 == 0, pltpu.roll(rotor, LANES - 1, 1), pltpu.roll(stator, 1, 1))
        return 0

    lax.fori_loop(0, 2, unpack, 0)

    def spatial(t, _):
        n, r = t // LAYERS, lax.rem(t, LAYERS)
        ghost = ghosts[n]
        here, sides = [], [[], [], []]
        for v in range(VARS):
            now = cells[n, v, r + 1, PAD:PAD + ROWS]
            here.append(now)
            sides[0].append((cells[n, v, r, PAD:PAD + ROWS], cells[n, v, r + 2, PAD:PAD + ROWS]))
            sides[1].append((cells[n, v, r + 1, PAD - 1:PAD + ROWS - 1], cells[n, v, r + 1, PAD + 1:PAD + ROWS + 1]))
            first = 63 - 2 * LAYERS * v
            placed = pltpu.roll(ghost, (first if first > 2 * LAYERS - 2 else first + LANES) - 2 * r, 1)
            lower = jnp.where(lane == 64, placed, jnp.where(lane == 0, 0.0, pltpu.roll(now, 1, 1)))
            upper = jnp.where(lane == 63, placed, jnp.where(lane == LANES - 1, 0.0, pltpu.roll(now, LANES - 1, 1)))
            sides[2].append((lower, upper))
        linear = [None] * VARS
        rest = [3.0 * now for now in here]
        for d in range(3):
            low0 = (0.25 * BEND[d]) * sides[d][0][0] + 0.5
            high0 = (0.25 * BEND[d]) * sides[d][0][1] - 0.5
            for v in range(VARS):
                low, high = sides[d][v]
                rest[v] = rest[v] + (high * high0 - low * low0)
                gap = high - low
                for u in range(VARS):
                    term = jac[d, u, v] * gap
                    linear[u] = term if linear[u] is None else linear[u] + term
        eddy = here[5]
        source = PRODUCE * eddy * jnp.sqrt(1.0 + here[1] * here[1] + here[2] * here[2]) - DESTROY * eddy * jnp.abs(eddy)
        rest[5] = rest[5] - source
        pace = step[r]
        for v in range(VARS):
            fresh[n, v, r] = here[v] - pace * (rest[v] + 0.5 * linear[v])
        return 0

    lax.fori_loop(0, 2 * LAYERS, spatial, 0)

    def finish(k, _):
        slot, g = 1 - k // GROUPS, lax.rem(k, GROUPS)
        wait_part(back_recv.at[slot * GROUPS + g])
        for pair in range(LAYERS // 2):
            r = 2 * pair + lax.rem(slot + 1 - rad, 2)
            scaled = step[r]
            for n in range(2):
                for i in range(TAKE):
                    v = g * TAKE + i
                    out[n, v, r] = fresh[n, v, r] - scaled * returned[n, v, r]
        return 0

    lax.fori_loop(0, 2 * GROUPS, finish, 0)
    whole = gathered.at[:, pl.ds(0, TIMES - 2)]
    pltpu.make_async_copy(whole, whole, out_send).wait()
    pltpu.make_async_copy(whole, whole, back_send).wait()
    for copy in side_copies:
        copy.wait_send()

    @pl.when(meets)
    def _():
        for swap in swaps:
            swap.wait_send()


def per_device(flow_state, pseudo_step, frequency, flux_jac, donor_offset):
    f32 = jnp.float32
    anywhere = pl.BlockSpec(memory_space=pl.ANY)
    scalar = pl.BlockSpec(memory_space=pltpu.SMEM)
    hbm = functools.partial(pltpu.with_memory_space_constraint, memory_space=pltpu.HBM)
    dma = pltpu.SemaphoreType.DMA
    return pl.pallas_call(
        kernel,
        name="pseudo_time_step",
        out_shape=pltpu.VMEM(flow_state.shape, f32),
        in_specs=[anywhere, anywhere, scalar, anywhere, anywhere],
        out_specs=pl.BlockSpec(memory_space=pltpu.VMEM),
        scratch_shapes=[
            pltpu.VMEM((2, VARS, LAYERS + 2, ROWS + 2 * PAD, LANES), f32),
            pltpu.VMEM((LAYERS, ROWS, LANES), f32),
            pltpu.SMEM((3, VARS, VARS), f32),
            pltpu.SMEM((TIMES,), jnp.int32),
            pltpu.VMEM((2, 2, VARS, LAYERS, LANES), f32),
            pltpu.VMEM((2, 2, VARS, LAYERS, LANES), f32),
            pltpu.VMEM((2, 3 * ROWS, LANES), f32),
            pltpu.VMEM((2, ROWS, LANES), f32),
            pltpu.VMEM((2, TIMES, VARS, TILE, LANES), f32),
            pltpu.VMEM((TIMES, VARS, TILE, LANES), f32),
            pltpu.VMEM((2, TIMES, VARS, TILE, LANES), f32),
            pltpu.VMEM((2, VARS, LAYERS, ROWS, LANES), f32),
            pltpu.VMEM((2, VARS, LAYERS, ROWS, LANES), f32),
            dma((6,)), dma, dma((2 * GROUPS,)), dma, dma((2 * GROUPS,)),
            dma((4,)), dma((4,)), dma((GROUPS,)), dma((GROUPS,)),
            pltpu.SemaphoreType.REGULAR,
        ],
        compiler_params=pltpu.CompilerParams(
            collective_id=0, has_side_effects=True, vmem_limit_bytes=40 << 20
        ),
        cost_estimate=pl.CostEstimate(flops=40_000_000, bytes_accessed=4_000_000, transcendentals=0),
    )(hbm(flow_state), hbm(pseudo_step), frequency, hbm(flux_jac), hbm(donor_offset))


def solution(mesh):
    return jax.shard_map(
        per_device,
        mesh=mesh,
        in_specs=(P("inst", None, "rad", "circ", None), P("rad", "circ", None), P(), P(), P()),
        out_specs=P("inst", None, "rad", "circ", None),
        check_vma=False,
    )
```

```python
import functools

import jax
import jax.numpy as jnp
import numpy as np
from jax import lax
from jax.experimental import pallas as pl
from jax.experimental.pallas import tpu as pltpu
from jax.sharding import PartitionSpec as P

MESH = pl.DeviceIdType.MESH
BEND = (0.3, 0.2, 0.25)
PRODUCE = 0.4
DESTROY = 0.2
VARS = 6
TIMES = 32
LAYERS = 8
ROWS = 32
TILE = 8
TAKE = 3
GROUPS = VARS // TAKE
LANES = 128
GROUP = 16
PAD = 8
FIRST = 1


def spectral_weights(length):
    k = np.arange(length)
    sign = np.where(k % 2 == 0, 1.0, -1.0)
    angle = np.pi * np.where(k == 0, 1, k) / length
    weights = 0.5 * sign / np.tan(angle)
    weights[0] = 0.0
    weights[length // 2] = 0.0
    return weights


def circulant(first, rows, fold):
    length = len(first)
    return [
        [first[n - m] if n >= m else fold * first[n - m + length] for m in range(length)]
        for n in range(rows)
    ]


def apply_rows(matrix, values):
    results = []
    for row in matrix:
        total = None
        for weight, value in zip(row, values):
            if abs(weight) < 1e-12:
                continue
            term = np.float32(weight) * value
            total = term if total is None else total + term
        results.append(total)
    return results


def differentiate(values):
    d = spectral_weights(TIMES)
    even = 0.5 * (d[:16] + d[16:])
    odd = 0.5 * (d[:16] - d[16:])
    even_even = 0.5 * (even[:8] + even[8:])
    even_odd = 0.5 * (even[:8] - even[8:])
    sums = [values[m] + values[m + 16] for m in range(16)]
    gaps = [values[m] - values[m + 16] for m in range(16)]
    sum_sums = [sums[m] + sums[m + 8] for m in range(8)]
    sum_gaps = [sums[m] - sums[m + 8] for m in range(8)]
    a = apply_rows(circulant(even_even, 8, 1.0), sum_sums)
    b = apply_rows(circulant(even_odd, 8, -1.0), sum_gaps)
    e = [a[n] + b[n] for n in range(8)] + [a[n] - b[n] for n in range(8)]
    o = apply_rows(circulant(odd, 16, -1.0), gaps)
    return [e[n] + o[n] for n in range(16)] + [e[n] - o[n] for n in range(16)]


def kernel(
    q, dt_hbm, freq, jac_hbm, shift_hbm, out,
    cells, step, jac, shift, rows_out, rows_in, columns, ghosts,
    gathered, beyond, derived, returned, fresh,
    local_sem, out_send, out_recv, back_send, back_recv, side_send, side_recv, swap_send, swap_recv, entered,
):
    me = lax.axis_index("inst")
    rad = lax.axis_index("rad")
    circ = lax.axis_index("circ")
    x, y, c = me // 8, lax.rem(me // 2, 4), lax.rem(me, 2)
    peers = []
    for dx, dy, dc in [
        (1, 2, 0), (1, 2, 1), (1, 1, 0), (1, 3, 0), (1, 1, 1), (1, 3, 1), (1, 0, 0), (1, 0, 1),
        (0, 2, 0), (0, 2, 1), (0, 1, 0), (0, 3, 0), (0, 1, 1), (0, 3, 1), (0, 0, 1),
    ]:
        px, py, pc = lax.rem(x + dx, 2), lax.rem(y + dy, 4), lax.rem(c + dc, 2)
        peers.append(((px * 4 + py) * 2 + pc, px * 4 + pc * 2, pl.multiple_of(py * TILE, TILE)))
    after = {"circ": lax.rem(circ + 1, 4)}
    before = {"circ": lax.rem(circ + 3, 4)}
    across = {"rad": 1 - rad, "inst": ((1 - x) * 4 + y) * 2 + 1 - c}
    meets = jnp.logical_and(x == 1 - rad, c == 1 - rad)

    barrier = pltpu.get_barrier_semaphore()
    for dx, dy in [(1, 2), (1, 1), (1, 3), (0, 2), (1, 0), (0, 1), (0, 3)]:
        chip = lax.rem(x + dx, 2) * 4 + lax.rem(y + dy, 4)
        pl.semaphore_signal(barrier, inc=1, device_id={"inst": 2 * chip}, device_id_type=MESH)

    @pl.when(c == 1)
    def _():
        pl.semaphore_signal(barrier, inc=1, device_id={"inst": me - c}, device_id_type=MESH)

    for axis, place, chip in (
        ("circ", after["circ"], me // 2),
        ("circ", before["circ"], me // 2),
        ("rad", 1 - rad, (1 - x) * 4 + y),
    ):
        pl.semaphore_signal(
            barrier, inc=1, device_id={axis: place, "inst": 2 * chip + 1}, device_id_type=MESH
        )

    my_layer, my_row = x * 4 + c * 2, pl.multiple_of(y * TILE, TILE)
    loads = [
        pltpu.make_async_copy(
            q.at[:, :, r], cells.at[:, :, r + 1, pl.ds(PAD, ROWS)], local_sem.at[0]
        )
        for r in range(LAYERS)
    ]
    for copy in loads:
        copy.start()
    small = [
        pltpu.make_async_copy(dt_hbm, step, local_sem.at[1]),
        pltpu.make_async_copy(jac_hbm, jac, local_sem.at[2]),
        pltpu.make_async_copy(shift_hbm, shift, local_sem.at[3]),
    ]
    for slot in range(2):
        small.append(
            pltpu.make_async_copy(
                q.at[:, :, my_layer + lax.rem(slot + 1 - rad, 2), pl.ds(my_row, TILE)],
                gathered.at[slot, pl.ds(2 * me, 2)], local_sem.at[4 + slot],
            )
        )
    for copy in small:
        copy.start()

    @pl.when(c == 0)
    def _():
        pl.semaphore_wait(barrier, GROUP - 1)
        pl.semaphore_signal(entered, inc=1, device_id={"inst": me + 1 - c}, device_id_type=MESH)

    @pl.when(c == 1)
    def _():
        pl.semaphore_wait(entered, 1)

    def send_out(k, _):
        slot, g = k // GROUPS, lax.rem(k, GROUPS)
        for peer, layer, row in peers:
            pltpu.make_async_remote_copy(
                q.at[:, pl.ds(g * TAKE, TAKE), layer + lax.rem(slot + 1 - rad, 2), pl.ds(row, TILE)],
                gathered.at[slot, pl.ds(2 * me, 2), pl.ds(g * TAKE, TAKE)],
                out_send, out_recv.at[k],
                device_id={"inst": peer}, device_id_type=MESH,
            ).start()
        return 0

    lax.fori_loop(0, 2 * GROUPS, send_out, 0)

    for copy in loads:
        copy.wait()

    lane = lax.broadcasted_iota(jnp.int32, (ROWS, LANES), 1)

    def pack(n, _):
        packed = jnp.zeros((ROWS, LANES), jnp.float32)
        for v in range(VARS):
            for r in range(LAYERS):
                rows_out[0, n, v, r:r + 1] = cells[n, v, r + 1, PAD + ROWS - 1:PAD + ROWS]
                rows_out[1, n, v, r:r + 1] = cells[n, v, r + 1, PAD:PAD + 1]
                j = v * LAYERS + r
                block = pltpu.roll(cells[n, v, r + 1, PAD:PAD + ROWS], (2 * j - 63) % LANES, 1)
                packed = jnp.where(lane // 2 == j, block, packed)
        columns[n, ROWS:2 * ROWS] = packed
        return 0

    lax.fori_loop(0, 2, pack, 0)
    side_copies = [
        pltpu.make_async_remote_copy(
            rows_out.at[0], rows_in.at[0], side_send.at[0], side_recv.at[0],
            device_id=after, device_id_type=MESH,
        ),
        pltpu.make_async_remote_copy(
            rows_out.at[1], rows_in.at[1], side_send.at[1], side_recv.at[1],
            device_id=before, device_id_type=MESH,
        ),
        pltpu.make_async_remote_copy(
            columns.at[:, pl.ds(ROWS, ROWS)], columns.at[:, pl.ds(0, ROWS)],
            side_send.at[2], side_recv.at[2], device_id=after, device_id_type=MESH,
        ),
        pltpu.make_async_remote_copy(
            columns.at[:, pl.ds(ROWS, ROWS)], columns.at[:, pl.ds(2 * ROWS, ROWS)],
            side_send.at[3], side_recv.at[3], device_id=before, device_id_type=MESH,
        ),
    ]

    @pl.when(c == 1)
    def _():
        pl.semaphore_wait(barrier, 6)
        pl.semaphore_signal(entered, inc=1, device_id={"inst": me - c}, device_id_type=MESH)

    @pl.when(c == 0)
    def _():
        pl.semaphore_wait(entered, 1)

    for copy in side_copies:
        copy.start()
    cells[:, :, 0, PAD:PAD + ROWS] = jnp.zeros((2, VARS, ROWS, LANES), jnp.float32)
    cells[:, :, LAYERS + 1, PAD:PAD + ROWS] = jnp.zeros((2, VARS, ROWS, LANES), jnp.float32)
    for copy in small:
        copy.wait()

    def wait_part(sem):
        part = gathered.at[0, pl.ds(0, TIMES - 2), pl.ds(0, TAKE)]
        pltpu.make_async_copy(part, part, sem).wait()

    swaps = [
        pltpu.make_async_remote_copy(
            gathered.at[0, :, pl.ds(g * TAKE, TAKE)], beyond.at[:, pl.ds(g * TAKE, TAKE)],
            swap_send.at[g], swap_recv.at[g], device_id=across, device_id_type=MESH,
        )
        for g in range(GROUPS)
    ]

    @pl.when(meets)
    def _():
        for g in range(GROUPS):
            wait_part(out_recv.at[g])
            swaps[g].start()

    pace = freq[0]
    side = (1 - 2 * rad).astype(jnp.float32)

    def radial_term(m, _):
        w = [beyond[m, v] for v in range(VARS)]
        curved = (0.25 * BEND[0]) * w[0]
        for u in range(VARS):
            total = curved * w[u]
            for v in range(VARS):
                total = total + (0.5 * jac[0, u, v]) * w[v]
            beyond[m, u] = side * total - 0.5 * w[u]
        return 0

    def which(k):
        return lax.rem(k // GROUPS + meets.astype(jnp.int32), 2), lax.rem(k, GROUPS)

    def post(k, early):
        slot, g = which(k)
        layer = my_layer + lax.rem(slot + 1 - rad, 2)
        for peer, _, _ in peers:
            enters_early = peer == FIRST

            @pl.when(enters_early if early else jnp.logical_not(enters_early))
            def _():
                pltpu.make_async_remote_copy(
                    derived.at[slot, pl.ds(2 * peer, 2), pl.ds(g * TAKE, TAKE)],
                    returned.at[:, pl.ds(g * TAKE, TAKE), layer, pl.ds(my_row, TILE)],
                    back_send, back_recv.at[slot * GROUPS + g],
                    device_id={"inst": peer}, device_id_type=MESH,
                ).start()

    def send_back(k, _):
        slot, g = which(k)
        meeting = jnp.logical_and(meets, slot == 0)

        @pl.when(jnp.logical_not(meeting))
        def _():
            wait_part(out_recv.at[slot * GROUPS + g])

        @pl.when(jnp.logical_and(meeting, g == 0))
        def _():
            for swap in swaps:
                swap.wait_recv()
            lax.fori_loop(0, TIMES, radial_term, 0)

        for i in range(TAKE):
            v = g * TAKE + i
            values = [gathered[slot, m, v] for m in range(TIMES)]
            for m, value in enumerate(differentiate(values)):
                derived[slot, m, v] = pace * value

        @pl.when(meeting)
        def _():
            for i in range(TAKE):
                v = g * TAKE + i
                for m in range(TIMES):
                    derived[0, m, v] = derived[0, m, v] + beyond[m, v]

        layer = my_layer + lax.rem(slot + 1 - rad, 2)
        for n in range(2):
            for i in range(TAKE):
                v = g * TAKE + i
                returned[n, v, layer, pl.ds(my_row, TILE)] = derived[slot, 2 * me + n, v]
        post(k, True)

        @pl.when(k > 0)
        def _():
            post(k - 1, False)

        return 0

    lax.fori_loop(0, 2 * GROUPS, send_back, 0)
    post(2 * GROUPS - 1, False)

    for copy in side_copies:
        copy.wait_recv()

    def unpack(n, _):
        for v in range(VARS):
            for r in range(LAYERS):
                cells[n, v, r + 1, PAD - 1:PAD] = rows_in[0, n, v, r:r + 1]
                cells[n, v, r + 1, PAD + ROWS:PAD + ROWS + 1] = rows_in[1, n, v, r:r + 1]
        s = shift[2 * me + n]
        stator = columns[n, pl.ds(ROWS + s, ROWS)]
        rotor = columns[n, pl.ds(ROWS - s, ROWS)]
        ghosts[n] = jnp.where(lane % 2 == 0, pltpu.roll(rotor, LANES - 1, 1), pltpu.roll(stator, 1, 1))
        return 0

    lax.fori_loop(0, 2, unpack, 0)

    def spatial(t, _):
        n, r = t // LAYERS, lax.rem(t, LAYERS)
        ghost = ghosts[n]
        here, sides = [], [[], [], []]
        for v in range(VARS):
            now = cells[n, v, r + 1, PAD:PAD + ROWS]
            here.append(now)
            sides[0].append((cells[n, v, r, PAD:PAD + ROWS], cells[n, v, r + 2, PAD:PAD + ROWS]))
            sides[1].append((cells[n, v, r + 1, PAD - 1:PAD + ROWS - 1], cells[n, v, r + 1, PAD + 1:PAD + ROWS + 1]))
            first = 63 - 2 * LAYERS * v
            placed = pltpu.roll(ghost, (first if first > 2 * LAYERS - 2 else first + LANES) - 2 * r, 1)
            lower = jnp.where(lane == 64, placed, jnp.where(lane == 0, 0.0, pltpu.roll(now, 1, 1)))
            upper = jnp.where(lane == 63, placed, jnp.where(lane == LANES - 1, 0.0, pltpu.roll(now, LANES - 1, 1)))
            sides[2].append((lower, upper))
        linear = [None] * VARS
        rest = [3.0 * now for now in here]
        for d in range(3):
            low0 = (0.25 * BEND[d]) * sides[d][0][0] + 0.5
            high0 = (0.25 * BEND[d]) * sides[d][0][1] - 0.5
            for v in range(VARS):
                low, high = sides[d][v]
                rest[v] = rest[v] + (high * high0 - low * low0)
                gap = high - low
                for u in range(VARS):
                    term = jac[d, u, v] * gap
                    linear[u] = term if linear[u] is None else linear[u] + term
        eddy = here[5]
        source = PRODUCE * eddy * jnp.sqrt(1.0 + here[1] * here[1] + here[2] * here[2]) - DESTROY * eddy * jnp.abs(eddy)
        rest[5] = rest[5] - source
        pace = step[r]
        for v in range(VARS):
            fresh[n, v, r] = here[v] - pace * (rest[v] + 0.5 * linear[v])
        return 0

    lax.fori_loop(0, 2 * LAYERS, spatial, 0)

    def finish(k, _):
        slot, g = 1 - k // GROUPS, lax.rem(k, GROUPS)
        wait_part(back_recv.at[slot * GROUPS + g])
        for pair in range(LAYERS // 2):
            r = 2 * pair + lax.rem(slot + 1 - rad, 2)
            scaled = step[r]
            for n in range(2):
                for i in range(TAKE):
                    v = g * TAKE + i
                    out[n, v, r] = fresh[n, v, r] - scaled * returned[n, v, r]
        return 0

    lax.fori_loop(0, 2 * GROUPS, finish, 0)
    whole = gathered.at[:, pl.ds(0, TIMES - 2)]
    pltpu.make_async_copy(whole, whole, out_send).wait()
    pltpu.make_async_copy(whole, whole, back_send).wait()
    for copy in side_copies:
        copy.wait_send()

    @pl.when(meets)
    def _():
        for swap in swaps:
            swap.wait_send()


def per_device(flow_state, pseudo_step, frequency, flux_jac, donor_offset):
    f32 = jnp.float32
    anywhere = pl.BlockSpec(memory_space=pl.ANY)
    scalar = pl.BlockSpec(memory_space=pltpu.SMEM)
    hbm = functools.partial(pltpu.with_memory_space_constraint, memory_space=pltpu.HBM)
    dma = pltpu.SemaphoreType.DMA
    return pl.pallas_call(
        kernel,
        name="pseudo_time_step",
        out_shape=pltpu.VMEM(flow_state.shape, f32),
        in_specs=[anywhere, anywhere, scalar, anywhere, anywhere],
        out_specs=pl.BlockSpec(memory_space=pltpu.VMEM),
        scratch_shapes=[
            pltpu.VMEM((2, VARS, LAYERS + 2, ROWS + 2 * PAD, LANES), f32),
            pltpu.VMEM((LAYERS, ROWS, LANES), f32),
            pltpu.SMEM((3, VARS, VARS), f32),
            pltpu.SMEM((TIMES,), jnp.int32),
            pltpu.VMEM((2, 2, VARS, LAYERS, LANES), f32),
            pltpu.VMEM((2, 2, VARS, LAYERS, LANES), f32),
            pltpu.VMEM((2, 3 * ROWS, LANES), f32),
            pltpu.VMEM((2, ROWS, LANES), f32),
            pltpu.VMEM((2, TIMES, VARS, TILE, LANES), f32),
            pltpu.VMEM((TIMES, VARS, TILE, LANES), f32),
            pltpu.VMEM((2, TIMES, VARS, TILE, LANES), f32),
            pltpu.VMEM((2, VARS, LAYERS, ROWS, LANES), f32),
            pltpu.VMEM((2, VARS, LAYERS, ROWS, LANES), f32),
            dma((6,)), dma, dma((2 * GROUPS,)), dma, dma((2 * GROUPS,)),
            dma((4,)), dma((4,)), dma((GROUPS,)), dma((GROUPS,)),
            pltpu.SemaphoreType.REGULAR,
        ],
        compiler_params=pltpu.CompilerParams(
            collective_id=0, has_side_effects=True, vmem_limit_bytes=40 << 20
        ),
        cost_estimate=pl.CostEstimate(flops=40_000_000, bytes_accessed=4_000_000, transcendentals=0),
    )(hbm(flow_state), hbm(pseudo_step), frequency, hbm(flux_jac), hbm(donor_offset))


def solution(mesh):
    return jax.shard_map(
        per_device,
        mesh=mesh,
        in_specs=(P("inst", None, "rad", "circ", None), P("rad", "circ", None), P(), P(), P()),
        out_specs=P("inst", None, "rad", "circ", None),
        check_vma=False,
    )
```

```python
import functools

import jax
import jax.numpy as jnp
import numpy as np
from jax import lax
from jax.experimental import pallas as pl
from jax.experimental.pallas import tpu as pltpu
from jax.sharding import PartitionSpec as P

MESH = pl.DeviceIdType.MESH
BEND = (0.3, 0.2, 0.25)
PRODUCE = 0.4
DESTROY = 0.2
VARS = 6
TIMES = 32
LAYERS = 8
ROWS = 32
TILE = 8
TAKE = 3
GROUPS = VARS // TAKE
LANES = 128
GROUP = 16
PAD = 8


def spectral_weights(length):
    k = np.arange(length)
    sign = np.where(k % 2 == 0, 1.0, -1.0)
    angle = np.pi * np.where(k == 0, 1, k) / length
    weights = 0.5 * sign / np.tan(angle)
    weights[0] = 0.0
    weights[length // 2] = 0.0
    return weights


def circulant(first, rows, fold):
    length = len(first)
    return [
        [first[n - m] if n >= m else fold * first[n - m + length] for m in range(length)]
        for n in range(rows)
    ]


def apply_rows(matrix, values):
    results = []
    for row in matrix:
        total = None
        for weight, value in zip(row, values):
            if abs(weight) < 1e-12:
                continue
            term = np.float32(weight) * value
            total = term if total is None else total + term
        results.append(total)
    return results


def differentiate(values):
    d = spectral_weights(TIMES)
    even = 0.5 * (d[:16] + d[16:])
    odd = 0.5 * (d[:16] - d[16:])
    even_even = 0.5 * (even[:8] + even[8:])
    even_odd = 0.5 * (even[:8] - even[8:])
    sums = [values[m] + values[m + 16] for m in range(16)]
    gaps = [values[m] - values[m + 16] for m in range(16)]
    sum_sums = [sums[m] + sums[m + 8] for m in range(8)]
    sum_gaps = [sums[m] - sums[m + 8] for m in range(8)]
    a = apply_rows(circulant(even_even, 8, 1.0), sum_sums)
    b = apply_rows(circulant(even_odd, 8, -1.0), sum_gaps)
    e = [a[n] + b[n] for n in range(8)] + [a[n] - b[n] for n in range(8)]
    o = apply_rows(circulant(odd, 16, -1.0), gaps)
    return [e[n] + o[n] for n in range(16)] + [e[n] - o[n] for n in range(16)]


def kernel(
    q, dt_hbm, freq, jac_hbm, shift_hbm, out,
    cells, step, jac, shift, rows_out, rows_in, columns, ghosts,
    gathered, beyond, derived, returned, fresh,
    local_sem, out_send, out_recv, back_send, back_recv, side_send, side_recv, swap_send, swap_recv, entered,
):
    me = lax.axis_index("inst")
    rad = lax.axis_index("rad")
    circ = lax.axis_index("circ")
    x, y, c = me // 8, lax.rem(me // 2, 4), lax.rem(me, 2)
    peers = []
    for dx, dy, dc in [
        (1, 2, 0), (1, 2, 1), (1, 1, 0), (1, 3, 0), (1, 1, 1), (1, 3, 1), (1, 0, 0), (1, 0, 1),
        (0, 2, 0), (0, 2, 1), (0, 1, 0), (0, 3, 0), (0, 1, 1), (0, 3, 1), (0, 0, 1),
    ]:
        px, py, pc = lax.rem(x + dx, 2), lax.rem(y + dy, 4), lax.rem(c + dc, 2)
        peers.append(((px * 4 + py) * 2 + pc, px * 4 + pc * 2, pl.multiple_of(py * TILE, TILE)))
    after = {"circ": lax.rem(circ + 1, 4)}
    before = {"circ": lax.rem(circ + 3, 4)}
    across = {"rad": 1 - rad, "inst": ((1 - x) * 4 + y) * 2 + 1 - c}
    meets = jnp.logical_and(x == 1 - rad, c == 1 - rad)

    barrier = pltpu.get_barrier_semaphore()
    for dx, dy in [(1, 2), (1, 1), (1, 3), (0, 2), (1, 0), (0, 1), (0, 3)]:
        chip = lax.rem(x + dx, 2) * 4 + lax.rem(y + dy, 4)
        pl.semaphore_signal(barrier, inc=1, device_id={"inst": 2 * chip}, device_id_type=MESH)

    @pl.when(c == 1)
    def _():
        pl.semaphore_signal(barrier, inc=1, device_id={"inst": me - c}, device_id_type=MESH)

    for axis, place, chip in (
        ("circ", after["circ"], me // 2),
        ("circ", before["circ"], me // 2),
        ("rad", 1 - rad, (1 - x) * 4 + y),
    ):
        pl.semaphore_signal(
            barrier, inc=1, device_id={axis: place, "inst": 2 * chip + 1}, device_id_type=MESH
        )

    my_layer, my_row = x * 4 + c * 2, pl.multiple_of(y * TILE, TILE)
    loads = [
        pltpu.make_async_copy(
            q.at[:, :, r], cells.at[:, :, r + 1, pl.ds(PAD, ROWS)], local_sem.at[0]
        )
        for r in range(LAYERS)
    ]
    for copy in loads:
        copy.start()
    small = [
        pltpu.make_async_copy(dt_hbm, step, local_sem.at[1]),
        pltpu.make_async_copy(jac_hbm, jac, local_sem.at[2]),
        pltpu.make_async_copy(shift_hbm, shift, local_sem.at[3]),
    ]
    for slot in range(2):
        small.append(
            pltpu.make_async_copy(
                q.at[:, :, my_layer + lax.rem(slot + 1 - rad, 2), pl.ds(my_row, TILE)],
                gathered.at[slot, pl.ds(2 * me, 2)], local_sem.at[4 + slot],
            )
        )
    for copy in small:
        copy.start()

    @pl.when(c == 0)
    def _():
        pl.semaphore_wait(barrier, GROUP - 1)
        pl.semaphore_signal(entered, inc=1, device_id={"inst": me + 1 - c}, device_id_type=MESH)

    @pl.when(c == 1)
    def _():
        pl.semaphore_wait(entered, 1)

    def send_out(k, _):
        slot, g = k // GROUPS, lax.rem(k, GROUPS)
        for peer, layer, row in peers:
            pltpu.make_async_remote_copy(
                q.at[:, pl.ds(g * TAKE, TAKE), layer + lax.rem(slot + 1 - rad, 2), pl.ds(row, TILE)],
                gathered.at[slot, pl.ds(2 * me, 2), pl.ds(g * TAKE, TAKE)],
                out_send, out_recv.at[k],
                device_id={"inst": peer}, device_id_type=MESH,
            ).start()
        return 0

    lax.fori_loop(0, 2 * GROUPS, send_out, 0)

    for copy in loads:
        copy.wait()

    lane = lax.broadcasted_iota(jnp.int32, (ROWS, LANES), 1)

    def pack(n, _):
        packed = jnp.zeros((ROWS, LANES), jnp.float32)
        for v in range(VARS):
            for r in range(LAYERS):
                rows_out[0, n, v, r:r + 1] = cells[n, v, r + 1, PAD + ROWS - 1:PAD + ROWS]
                rows_out[1, n, v, r:r + 1] = cells[n, v, r + 1, PAD:PAD + 1]
                j = v * LAYERS + r
                block = pltpu.roll(cells[n, v, r + 1, PAD:PAD + ROWS], (2 * j - 63) % LANES, 1)
                packed = jnp.where(lane // 2 == j, block, packed)
        columns[n, ROWS:2 * ROWS] = packed
        return 0

    lax.fori_loop(0, 2, pack, 0)
    side_copies = [
        pltpu.make_async_remote_copy(
            rows_out.at[0], rows_in.at[0], side_send.at[0], side_recv.at[0],
            device_id=after, device_id_type=MESH,
        ),
        pltpu.make_async_remote_copy(
            rows_out.at[1], rows_in.at[1], side_send.at[1], side_recv.at[1],
            device_id=before, device_id_type=MESH,
        ),
        pltpu.make_async_remote_copy(
            columns.at[:, pl.ds(ROWS, ROWS)], columns.at[:, pl.ds(0, ROWS)],
            side_send.at[2], side_recv.at[2], device_id=after, device_id_type=MESH,
        ),
        pltpu.make_async_remote_copy(
            columns.at[:, pl.ds(ROWS, ROWS)], columns.at[:, pl.ds(2 * ROWS, ROWS)],
            side_send.at[3], side_recv.at[3], device_id=before, device_id_type=MESH,
        ),
    ]

    @pl.when(c == 1)
    def _():
        pl.semaphore_wait(barrier, 6)
        pl.semaphore_signal(entered, inc=1, device_id={"inst": me - c}, device_id_type=MESH)

    @pl.when(c == 0)
    def _():
        pl.semaphore_wait(entered, 1)

    for copy in side_copies:
        copy.start()
    cells[:, :, 0, PAD:PAD + ROWS] = jnp.zeros((2, VARS, ROWS, LANES), jnp.float32)
    cells[:, :, LAYERS + 1, PAD:PAD + ROWS] = jnp.zeros((2, VARS, ROWS, LANES), jnp.float32)
    for copy in small:
        copy.wait()

    def wait_part(sem):
        part = gathered.at[0, pl.ds(0, TIMES - 2), pl.ds(0, TAKE)]
        pltpu.make_async_copy(part, part, sem).wait()

    swaps = [
        pltpu.make_async_remote_copy(
            gathered.at[0, :, pl.ds(g * TAKE, TAKE)], beyond.at[:, pl.ds(g * TAKE, TAKE)],
            swap_send.at[g], swap_recv.at[g], device_id=across, device_id_type=MESH,
        )
        for g in range(GROUPS)
    ]

    @pl.when(meets)
    def _():
        for g in range(GROUPS):
            wait_part(out_recv.at[g])
            swaps[g].start()

    pace = freq[0]
    side = (1 - 2 * rad).astype(jnp.float32)

    def radial_term(m, _):
        w = [beyond[m, v] for v in range(VARS)]
        curved = (0.25 * BEND[0]) * w[0]
        for u in range(VARS):
            total = curved * w[u]
            for v in range(VARS):
                total = total + (0.5 * jac[0, u, v]) * w[v]
            beyond[m, u] = side * total - 0.5 * w[u]
        return 0

    def which(k):
        return lax.rem(k // GROUPS + meets.astype(jnp.int32), 2), lax.rem(k, GROUPS)

    def post(k, early):
        slot, g = which(k)
        layer = my_layer + lax.rem(slot + 1 - rad, 2)
        for peer, _, _ in peers:
            enters_early = lax.rem(peer, 2) == 1

            @pl.when(enters_early if early else jnp.logical_not(enters_early))
            def _():
                pltpu.make_async_remote_copy(
                    derived.at[slot, pl.ds(2 * peer, 2), pl.ds(g * TAKE, TAKE)],
                    returned.at[:, pl.ds(g * TAKE, TAKE), layer, pl.ds(my_row, TILE)],
                    back_send, back_recv.at[slot * GROUPS + g],
                    device_id={"inst": peer}, device_id_type=MESH,
                ).start()

    def send_back(k, _):
        slot, g = which(k)
        meeting = jnp.logical_and(meets, slot == 0)

        @pl.when(jnp.logical_not(meeting))
        def _():
            wait_part(out_recv.at[slot * GROUPS + g])

        @pl.when(jnp.logical_and(meeting, g == 0))
        def _():
            for swap in swaps:
                swap.wait_recv()
            lax.fori_loop(0, TIMES, radial_term, 0)

        for i in range(TAKE):
            v = g * TAKE + i
            values = [gathered[slot, m, v] for m in range(TIMES)]
            for m, value in enumerate(differentiate(values)):
                derived[slot, m, v] = pace * value

        @pl.when(meeting)
        def _():
            for i in range(TAKE):
                v = g * TAKE + i
                for m in range(TIMES):
                    derived[0, m, v] = derived[0, m, v] + beyond[m, v]

        layer = my_layer + lax.rem(slot + 1 - rad, 2)
        for n in range(2):
            for i in range(TAKE):
                v = g * TAKE + i
                returned[n, v, layer, pl.ds(my_row, TILE)] = derived[slot, 2 * me + n, v]
        post(k, True)

        @pl.when(k > 0)
        def _():
            post(k - 1, False)

        return 0

    lax.fori_loop(0, 2 * GROUPS, send_back, 0)
    post(2 * GROUPS - 1, False)

    for copy in side_copies:
        copy.wait_recv()

    def unpack(n, _):
        for v in range(VARS):
            for r in range(LAYERS):
                cells[n, v, r + 1, PAD - 1:PAD] = rows_in[0, n, v, r:r + 1]
                cells[n, v, r + 1, PAD + ROWS:PAD + ROWS + 1] = rows_in[1, n, v, r:r + 1]
        s = shift[2 * me + n]
        stator = columns[n, pl.ds(ROWS + s, ROWS)]
        rotor = columns[n, pl.ds(ROWS - s, ROWS)]
        ghosts[n] = jnp.where(lane % 2 == 0, pltpu.roll(rotor, LANES - 1, 1), pltpu.roll(stator, 1, 1))
        return 0

    lax.fori_loop(0, 2, unpack, 0)

    def spatial(t, _):
        n, r = t // LAYERS, lax.rem(t, LAYERS)
        ghost = ghosts[n]
        here, sides = [], [[], [], []]
        for v in range(VARS):
            now = cells[n, v, r + 1, PAD:PAD + ROWS]
            here.append(now)
            sides[0].append((cells[n, v, r, PAD:PAD + ROWS], cells[n, v, r + 2, PAD:PAD + ROWS]))
            sides[1].append((cells[n, v, r + 1, PAD - 1:PAD + ROWS - 1], cells[n, v, r + 1, PAD + 1:PAD + ROWS + 1]))
            first = 63 - 2 * LAYERS * v
            placed = pltpu.roll(ghost, (first if first > 2 * LAYERS - 2 else first + LANES) - 2 * r, 1)
            lower = jnp.where(lane == 64, placed, jnp.where(lane == 0, 0.0, pltpu.roll(now, 1, 1)))
            upper = jnp.where(lane == 63, placed, jnp.where(lane == LANES - 1, 0.0, pltpu.roll(now, LANES - 1, 1)))
            sides[2].append((lower, upper))
        linear = [None] * VARS
        rest = [3.0 * now for now in here]
        for d in range(3):
            low0 = (0.25 * BEND[d]) * sides[d][0][0] + 0.5
            high0 = (0.25 * BEND[d]) * sides[d][0][1] - 0.5
            for v in range(VARS):
                low, high = sides[d][v]
                rest[v] = rest[v] + (high * high0 - low * low0)
                gap = high - low
                for u in range(VARS):
                    term = jac[d, u, v] * gap
                    linear[u] = term if linear[u] is None else linear[u] + term
        eddy = here[5]
        source = PRODUCE * eddy * jnp.sqrt(1.0 + here[1] * here[1] + here[2] * here[2]) - DESTROY * eddy * jnp.abs(eddy)
        rest[5] = rest[5] - source
        pace = step[r]
        for v in range(VARS):
            fresh[n, v, r] = here[v] - pace * (rest[v] + 0.5 * linear[v])
        return 0

    lax.fori_loop(0, 2 * LAYERS, spatial, 0)

    def finish(k, _):
        slot, g = 1 - k // GROUPS, lax.rem(k, GROUPS)
        wait_part(back_recv.at[slot * GROUPS + g])
        for pair in range(LAYERS // 2):
            r = 2 * pair + lax.rem(slot + 1 - rad, 2)
            scaled = step[r]
            for n in range(2):
                for i in range(TAKE):
                    v = g * TAKE + i
                    out[n, v, r] = fresh[n, v, r] - scaled * returned[n, v, r]
        return 0

    lax.fori_loop(0, 2 * GROUPS, finish, 0)
    whole = gathered.at[:, pl.ds(0, TIMES - 2)]
    pltpu.make_async_copy(whole, whole, out_send).wait()
    pltpu.make_async_copy(whole, whole, back_send).wait()
    for copy in side_copies:
        copy.wait_send()

    @pl.when(meets)
    def _():
        for swap in swaps:
            swap.wait_send()


def per_device(flow_state, pseudo_step, frequency, flux_jac, donor_offset):
    f32 = jnp.float32
    anywhere = pl.BlockSpec(memory_space=pl.ANY)
    scalar = pl.BlockSpec(memory_space=pltpu.SMEM)
    hbm = functools.partial(pltpu.with_memory_space_constraint, memory_space=pltpu.HBM)
    dma = pltpu.SemaphoreType.DMA
    return pl.pallas_call(
        kernel,
        name="pseudo_time_step",
        out_shape=pltpu.VMEM(flow_state.shape, f32),
        in_specs=[anywhere, anywhere, scalar, anywhere, anywhere],
        out_specs=pl.BlockSpec(memory_space=pltpu.VMEM),
        scratch_shapes=[
            pltpu.VMEM((2, VARS, LAYERS + 2, ROWS + 2 * PAD, LANES), f32),
            pltpu.VMEM((LAYERS, ROWS, LANES), f32),
            pltpu.SMEM((3, VARS, VARS), f32),
            pltpu.SMEM((TIMES,), jnp.int32),
            pltpu.VMEM((2, 2, VARS, LAYERS, LANES), f32),
            pltpu.VMEM((2, 2, VARS, LAYERS, LANES), f32),
            pltpu.VMEM((2, 3 * ROWS, LANES), f32),
            pltpu.VMEM((2, ROWS, LANES), f32),
            pltpu.VMEM((2, TIMES, VARS, TILE, LANES), f32),
            pltpu.VMEM((TIMES, VARS, TILE, LANES), f32),
            pltpu.VMEM((2, TIMES, VARS, TILE, LANES), f32),
            pltpu.VMEM((2, VARS, LAYERS, ROWS, LANES), f32),
            pltpu.VMEM((2, VARS, LAYERS, ROWS, LANES), f32),
            dma((6,)), dma, dma((2 * GROUPS,)), dma, dma((2 * GROUPS,)),
            dma((4,)), dma((4,)), dma((GROUPS,)), dma((GROUPS,)),
            pltpu.SemaphoreType.REGULAR,
        ],
        compiler_params=pltpu.CompilerParams(
            collective_id=0, has_side_effects=True, vmem_limit_bytes=40 << 20
        ),
        cost_estimate=pl.CostEstimate(flops=40_000_000, bytes_accessed=4_000_000, transcendentals=0),
    )(hbm(flow_state), hbm(pseudo_step), frequency, hbm(flux_jac), hbm(donor_offset))


def solution(mesh):
    return jax.shard_map(
        per_device,
        mesh=mesh,
        in_specs=(P("inst", None, "rad", "circ", None), P("rad", "circ", None), P(), P(), P()),
        out_specs=P("inst", None, "rad", "circ", None),
        check_vma=False,
    )
```

```python
import functools

import jax
import jax.numpy as jnp
import numpy as np
from jax import lax
from jax.experimental import pallas as pl
from jax.experimental.pallas import tpu as pltpu
from jax.sharding import PartitionSpec as P

MESH = pl.DeviceIdType.MESH
BEND = (0.3, 0.2, 0.25)
PRODUCE = 0.4
DESTROY = 0.2
VARS = 6
TIMES = 32
LAYERS = 8
ROWS = 32
TILE = 8
TAKE = 2
GROUPS = VARS // TAKE
LANES = 128
GROUP = 16
PAD = 8


def spectral_weights(length):
    k = np.arange(length)
    sign = np.where(k % 2 == 0, 1.0, -1.0)
    angle = np.pi * np.where(k == 0, 1, k) / length
    weights = 0.5 * sign / np.tan(angle)
    weights[0] = 0.0
    weights[length // 2] = 0.0
    return weights


def circulant(first, rows, fold):
    length = len(first)
    return [
        [first[n - m] if n >= m else fold * first[n - m + length] for m in range(length)]
        for n in range(rows)
    ]


def apply_rows(matrix, values):
    results = []
    for row in matrix:
        total = None
        for weight, value in zip(row, values):
            if abs(weight) < 1e-12:
                continue
            term = np.float32(weight) * value
            total = term if total is None else total + term
        results.append(total)
    return results


def differentiate(values):
    d = spectral_weights(TIMES)
    even = 0.5 * (d[:16] + d[16:])
    odd = 0.5 * (d[:16] - d[16:])
    even_even = 0.5 * (even[:8] + even[8:])
    even_odd = 0.5 * (even[:8] - even[8:])
    sums = [values[m] + values[m + 16] for m in range(16)]
    gaps = [values[m] - values[m + 16] for m in range(16)]
    sum_sums = [sums[m] + sums[m + 8] for m in range(8)]
    sum_gaps = [sums[m] - sums[m + 8] for m in range(8)]
    a = apply_rows(circulant(even_even, 8, 1.0), sum_sums)
    b = apply_rows(circulant(even_odd, 8, -1.0), sum_gaps)
    e = [a[n] + b[n] for n in range(8)] + [a[n] - b[n] for n in range(8)]
    o = apply_rows(circulant(odd, 16, -1.0), gaps)
    return [e[n] + o[n] for n in range(16)] + [e[n] - o[n] for n in range(16)]


def kernel(
    q, dt_hbm, freq, jac_hbm, shift_hbm, out,
    cells, step, jac, shift, rows_out, rows_in, columns, ghosts,
    gathered, beyond, derived, returned, fresh,
    local_sem, out_send, out_recv, back_send, back_recv, side_send, side_recv, swap_send, swap_recv, entered,
):
    me = lax.axis_index("inst")
    rad = lax.axis_index("rad")
    circ = lax.axis_index("circ")
    x, y, c = me // 8, lax.rem(me // 2, 4), lax.rem(me, 2)
    peers = []
    for dx, dy, dc in [
        (1, 2, 0), (1, 2, 1), (1, 1, 0), (1, 3, 0), (1, 1, 1), (1, 3, 1), (1, 0, 0), (1, 0, 1),
        (0, 2, 0), (0, 2, 1), (0, 1, 0), (0, 3, 0), (0, 1, 1), (0, 3, 1), (0, 0, 1),
    ]:
        px, py, pc = lax.rem(x + dx, 2), lax.rem(y + dy, 4), lax.rem(c + dc, 2)
        peers.append(((px * 4 + py) * 2 + pc, px * 4 + pc * 2, pl.multiple_of(py * TILE, TILE)))
    after = {"circ": lax.rem(circ + 1, 4)}
    before = {"circ": lax.rem(circ + 3, 4)}
    across = {"rad": 1 - rad, "inst": ((1 - x) * 4 + y) * 2 + 1 - c}
    meets = jnp.logical_and(x == 1 - rad, c == 1 - rad)

    barrier = pltpu.get_barrier_semaphore()
    for dx, dy in [(1, 2), (1, 1), (1, 3), (0, 2), (1, 0), (0, 1), (0, 3)]:
        chip = lax.rem(x + dx, 2) * 4 + lax.rem(y + dy, 4)
        pl.semaphore_signal(barrier, inc=1, device_id={"inst": 2 * chip}, device_id_type=MESH)

    @pl.when(c == 1)
    def _():
        pl.semaphore_signal(barrier, inc=1, device_id={"inst": me - c}, device_id_type=MESH)

    for axis, place, chip in (
        ("circ", after["circ"], me // 2),
        ("circ", before["circ"], me // 2),
        ("rad", 1 - rad, (1 - x) * 4 + y),
    ):
        pl.semaphore_signal(
            barrier, inc=1, device_id={axis: place, "inst": 2 * chip + 1}, device_id_type=MESH
        )

    my_layer, my_row = x * 4 + c * 2, pl.multiple_of(y * TILE, TILE)
    loads = [
        pltpu.make_async_copy(
            q.at[:, :, r], cells.at[:, :, r + 1, pl.ds(PAD, ROWS)], local_sem.at[0]
        )
        for r in range(LAYERS)
    ]
    for copy in loads:
        copy.start()
    small = [
        pltpu.make_async_copy(dt_hbm, step, local_sem.at[1]),
        pltpu.make_async_copy(jac_hbm, jac, local_sem.at[2]),
        pltpu.make_async_copy(shift_hbm, shift, local_sem.at[3]),
    ]
    for slot in range(2):
        small.append(
            pltpu.make_async_copy(
                q.at[:, :, my_layer + lax.rem(slot + 1 - rad, 2), pl.ds(my_row, TILE)],
                gathered.at[slot, pl.ds(2 * me, 2)], local_sem.at[4 + slot],
            )
        )
    for copy in small:
        copy.start()

    @pl.when(c == 0)
    def _():
        pl.semaphore_wait(barrier, GROUP - 1)
        pl.semaphore_signal(entered, inc=1, device_id={"inst": me + 1 - c}, device_id_type=MESH)

    @pl.when(c == 1)
    def _():
        pl.semaphore_wait(entered, 1)

    def send_out(k, _):
        slot, g = k // GROUPS, lax.rem(k, GROUPS)
        for peer, layer, row in peers:
            pltpu.make_async_remote_copy(
                q.at[:, pl.ds(g * TAKE, TAKE), layer + lax.rem(slot + 1 - rad, 2), pl.ds(row, TILE)],
                gathered.at[slot, pl.ds(2 * me, 2), pl.ds(g * TAKE, TAKE)],
                out_send, out_recv.at[k],
                device_id={"inst": peer}, device_id_type=MESH,
            ).start()
        return 0

    lax.fori_loop(0, 2 * GROUPS, send_out, 0)

    for copy in loads:
        copy.wait()

    lane = lax.broadcasted_iota(jnp.int32, (ROWS, LANES), 1)

    def pack(n, _):
        packed = jnp.zeros((ROWS, LANES), jnp.float32)
        for v in range(VARS):
            for r in range(LAYERS):
                rows_out[0, n, v, r:r + 1] = cells[n, v, r + 1, PAD + ROWS - 1:PAD + ROWS]
                rows_out[1, n, v, r:r + 1] = cells[n, v, r + 1, PAD:PAD + 1]
                j = v * LAYERS + r
                block = pltpu.roll(cells[n, v, r + 1, PAD:PAD + ROWS], (2 * j - 63) % LANES, 1)
                packed = jnp.where(lane // 2 == j, block, packed)
        columns[n, ROWS:2 * ROWS] = packed
        return 0

    lax.fori_loop(0, 2, pack, 0)
    side_copies = [
        pltpu.make_async_remote_copy(
            rows_out.at[0], rows_in.at[0], side_send.at[0], side_recv.at[0],
            device_id=after, device_id_type=MESH,
        ),
        pltpu.make_async_remote_copy(
            rows_out.at[1], rows_in.at[1], side_send.at[1], side_recv.at[1],
            device_id=before, device_id_type=MESH,
        ),
        pltpu.make_async_remote_copy(
            columns.at[:, pl.ds(ROWS, ROWS)], columns.at[:, pl.ds(0, ROWS)],
            side_send.at[2], side_recv.at[2], device_id=after, device_id_type=MESH,
        ),
        pltpu.make_async_remote_copy(
            columns.at[:, pl.ds(ROWS, ROWS)], columns.at[:, pl.ds(2 * ROWS, ROWS)],
            side_send.at[3], side_recv.at[3], device_id=before, device_id_type=MESH,
        ),
    ]

    @pl.when(c == 1)
    def _():
        pl.semaphore_wait(barrier, 6)
        pl.semaphore_signal(entered, inc=1, device_id={"inst": me - c}, device_id_type=MESH)

    @pl.when(c == 0)
    def _():
        pl.semaphore_wait(entered, 1)

    for copy in side_copies:
        copy.start()
    cells[:, :, 0, PAD:PAD + ROWS] = jnp.zeros((2, VARS, ROWS, LANES), jnp.float32)
    cells[:, :, LAYERS + 1, PAD:PAD + ROWS] = jnp.zeros((2, VARS, ROWS, LANES), jnp.float32)
    for copy in small:
        copy.wait()

    def wait_part(sem):
        part = gathered.at[0, pl.ds(0, TIMES - 2), pl.ds(0, TAKE)]
        pltpu.make_async_copy(part, part, sem).wait()

    swaps = [
        pltpu.make_async_remote_copy(
            gathered.at[0, :, pl.ds(g * TAKE, TAKE)], beyond.at[:, pl.ds(g * TAKE, TAKE)],
            swap_send.at[g], swap_recv.at[g], device_id=across, device_id_type=MESH,
        )
        for g in range(GROUPS)
    ]

    @pl.when(meets)
    def _():
        for g in range(GROUPS):
            wait_part(out_recv.at[g])
            swaps[g].start()

    pace = freq[0]
    side = (1 - 2 * rad).astype(jnp.float32)

    def radial_term(m, _):
        w = [beyond[m, v] for v in range(VARS)]
        curved = (0.25 * BEND[0]) * w[0]
        for u in range(VARS):
            total = curved * w[u]
            for v in range(VARS):
                total = total + (0.5 * jac[0, u, v]) * w[v]
            beyond[m, u] = side * total - 0.5 * w[u]
        return 0

    def which(k):
        return lax.rem(k // GROUPS + meets.astype(jnp.int32), 2), lax.rem(k, GROUPS)

    def post(k, early):
        slot, g = which(k)
        layer = my_layer + lax.rem(slot + 1 - rad, 2)
        for peer, _, _ in peers:
            enters_early = lax.rem(peer, 2) == 1

            @pl.when(enters_early if early else jnp.logical_not(enters_early))
            def _():
                pltpu.make_async_remote_copy(
                    derived.at[slot, pl.ds(2 * peer, 2), pl.ds(g * TAKE, TAKE)],
                    returned.at[:, pl.ds(g * TAKE, TAKE), layer, pl.ds(my_row, TILE)],
                    back_send, back_recv.at[slot * GROUPS + g],
                    device_id={"inst": peer}, device_id_type=MESH,
                ).start()

    def send_back(k, _):
        slot, g = which(k)
        meeting = jnp.logical_and(meets, slot == 0)

        @pl.when(jnp.logical_not(meeting))
        def _():
            wait_part(out_recv.at[slot * GROUPS + g])

        @pl.when(jnp.logical_and(meeting, g == 0))
        def _():
            for swap in swaps:
                swap.wait_recv()
            lax.fori_loop(0, TIMES, radial_term, 0)

        for i in range(TAKE):
            v = g * TAKE + i
            values = [gathered[slot, m, v] for m in range(TIMES)]
            for m, value in enumerate(differentiate(values)):
                derived[slot, m, v] = pace * value

        @pl.when(meeting)
        def _():
            for i in range(TAKE):
                v = g * TAKE + i
                for m in range(TIMES):
                    derived[0, m, v] = derived[0, m, v] + beyond[m, v]

        layer = my_layer + lax.rem(slot + 1 - rad, 2)
        for n in range(2):
            for i in range(TAKE):
                v = g * TAKE + i
                returned[n, v, layer, pl.ds(my_row, TILE)] = derived[slot, 2 * me + n, v]
        post(k, True)

        @pl.when(k > 0)
        def _():
            post(k - 1, False)

        return 0

    lax.fori_loop(0, 2 * GROUPS, send_back, 0)
    post(2 * GROUPS - 1, False)

    for copy in side_copies:
        copy.wait_recv()

    def unpack(n, _):
        for v in range(VARS):
            for r in range(LAYERS):
                cells[n, v, r + 1, PAD - 1:PAD] = rows_in[0, n, v, r:r + 1]
                cells[n, v, r + 1, PAD + ROWS:PAD + ROWS + 1] = rows_in[1, n, v, r:r + 1]
        s = shift[2 * me + n]
        stator = columns[n, pl.ds(ROWS + s, ROWS)]
        rotor = columns[n, pl.ds(ROWS - s, ROWS)]
        ghosts[n] = jnp.where(lane % 2 == 0, pltpu.roll(rotor, LANES - 1, 1), pltpu.roll(stator, 1, 1))
        return 0

    lax.fori_loop(0, 2, unpack, 0)

    def spatial(t, _):
        n, r = t // LAYERS, lax.rem(t, LAYERS)
        ghost = ghosts[n]
        here, sides = [], [[], [], []]
        for v in range(VARS):
            now = cells[n, v, r + 1, PAD:PAD + ROWS]
            here.append(now)
            sides[0].append((cells[n, v, r, PAD:PAD + ROWS], cells[n, v, r + 2, PAD:PAD + ROWS]))
            sides[1].append((cells[n, v, r + 1, PAD - 1:PAD + ROWS - 1], cells[n, v, r + 1, PAD + 1:PAD + ROWS + 1]))
            first = 63 - 2 * LAYERS * v
            placed = pltpu.roll(ghost, (first if first > 2 * LAYERS - 2 else first + LANES) - 2 * r, 1)
            lower = jnp.where(lane == 64, placed, jnp.where(lane == 0, 0.0, pltpu.roll(now, 1, 1)))
            upper = jnp.where(lane == 63, placed, jnp.where(lane == LANES - 1, 0.0, pltpu.roll(now, LANES - 1, 1)))
            sides[2].append((lower, upper))
        linear = [None] * VARS
        rest = [3.0 * now for now in here]
        for d in range(3):
            low0 = (0.25 * BEND[d]) * sides[d][0][0] + 0.5
            high0 = (0.25 * BEND[d]) * sides[d][0][1] - 0.5
            for v in range(VARS):
                low, high = sides[d][v]
                rest[v] = rest[v] + (high * high0 - low * low0)
                gap = high - low
                for u in range(VARS):
                    term = jac[d, u, v] * gap
                    linear[u] = term if linear[u] is None else linear[u] + term
        eddy = here[5]
        source = PRODUCE * eddy * jnp.sqrt(1.0 + here[1] * here[1] + here[2] * here[2]) - DESTROY * eddy * jnp.abs(eddy)
        rest[5] = rest[5] - source
        pace = step[r]
        for v in range(VARS):
            fresh[n, v, r] = here[v] - pace * (rest[v] + 0.5 * linear[v])
        return 0

    lax.fori_loop(0, 2 * LAYERS, spatial, 0)

    def finish(k, _):
        slot, g = 1 - k // GROUPS, lax.rem(k, GROUPS)
        wait_part(back_recv.at[slot * GROUPS + g])
        for pair in range(LAYERS // 2):
            r = 2 * pair + lax.rem(slot + 1 - rad, 2)
            scaled = step[r]
            for n in range(2):
                for i in range(TAKE):
                    v = g * TAKE + i
                    out[n, v, r] = fresh[n, v, r] - scaled * returned[n, v, r]
        return 0

    lax.fori_loop(0, 2 * GROUPS, finish, 0)
    whole = gathered.at[:, pl.ds(0, TIMES - 2)]
    pltpu.make_async_copy(whole, whole, out_send).wait()
    pltpu.make_async_copy(whole, whole, back_send).wait()
    for copy in side_copies:
        copy.wait_send()

    @pl.when(meets)
    def _():
        for swap in swaps:
            swap.wait_send()


def per_device(flow_state, pseudo_step, frequency, flux_jac, donor_offset):
    f32 = jnp.float32
    anywhere = pl.BlockSpec(memory_space=pl.ANY)
    scalar = pl.BlockSpec(memory_space=pltpu.SMEM)
    hbm = functools.partial(pltpu.with_memory_space_constraint, memory_space=pltpu.HBM)
    dma = pltpu.SemaphoreType.DMA
    return pl.pallas_call(
        kernel,
        name="pseudo_time_step",
        out_shape=pltpu.VMEM(flow_state.shape, f32),
        in_specs=[anywhere, anywhere, scalar, anywhere, anywhere],
        out_specs=pl.BlockSpec(memory_space=pltpu.VMEM),
        scratch_shapes=[
            pltpu.VMEM((2, VARS, LAYERS + 2, ROWS + 2 * PAD, LANES), f32),
            pltpu.VMEM((LAYERS, ROWS, LANES), f32),
            pltpu.SMEM((3, VARS, VARS), f32),
            pltpu.SMEM((TIMES,), jnp.int32),
            pltpu.VMEM((2, 2, VARS, LAYERS, LANES), f32),
            pltpu.VMEM((2, 2, VARS, LAYERS, LANES), f32),
            pltpu.VMEM((2, 3 * ROWS, LANES), f32),
            pltpu.VMEM((2, ROWS, LANES), f32),
            pltpu.VMEM((2, TIMES, VARS, TILE, LANES), f32),
            pltpu.VMEM((TIMES, VARS, TILE, LANES), f32),
            pltpu.VMEM((2, TIMES, VARS, TILE, LANES), f32),
            pltpu.VMEM((2, VARS, LAYERS, ROWS, LANES), f32),
            pltpu.VMEM((2, VARS, LAYERS, ROWS, LANES), f32),
            dma((6,)), dma, dma((2 * GROUPS,)), dma, dma((2 * GROUPS,)),
            dma((4,)), dma((4,)), dma((GROUPS,)), dma((GROUPS,)),
            pltpu.SemaphoreType.REGULAR,
        ],
        compiler_params=pltpu.CompilerParams(
            collective_id=0, has_side_effects=True, vmem_limit_bytes=40 << 20
        ),
        cost_estimate=pl.CostEstimate(flops=40_000_000, bytes_accessed=4_000_000, transcendentals=0),
    )(hbm(flow_state), hbm(pseudo_step), frequency, hbm(flux_jac), hbm(donor_offset))


def solution(mesh):
    return jax.shard_map(
        per_device,
        mesh=mesh,
        in_specs=(P("inst", None, "rad", "circ", None), P("rad", "circ", None), P(), P(), P()),
        out_specs=P("inst", None, "rad", "circ", None),
        check_vma=False,
    )
```
